256 devices in a mesh: row: 32 (over x, z), col: 8 (over y, core).
Axes of the slice: x: 4, y: 4, z: 8, core: 2. Of those that a mesh axis runs over, the one named last changes fastest.
Arguments:
- momentum: float32 [2, 7168, 2048], P(None, 'row', 'col'), may hold values from -6 to 6
- gradient: bfloat16 [2, 7168, 2048], P(None, 'row', 'col'), may hold values from -6 to 6
- basis_in: bfloat16 [2, 2048, 512], P(None, 'col'), may hold values from -0.125 to 0.125
Outputs:
- momentum_new: float32 [2, 7168, 2048], P(None, 'row', 'col')
- direction: bfloat16 [2, 7168, 2048], P(None, 'row', 'col')
The draws below stay inside these ranges and needn't reach their ends.
All inputs are finite; a program needn't handle non-finite values.
Results may differ from the reference program's by a relative error of at most 0.02.
Values may be sent and summed in bfloat16 or wider, within the bound.
No kernel may reach another device: no remote copies, remote signals or barrier semaphores. Data moves between devices by JAX's collectives and lax.ppermute only.
A program may use at most 64 MiB of HBM per device.

```python
import math
import jax
import jax.numpy as jnp
from jax import lax

ROWS = 7168
COLS = 2048
RANK = 512
EXPERTS = 2


def block_scale(key, shape, split, smallest, high):
    def one(position, shards_of):
        steps = jax.random.uniform(jax.random.fold_in(jax.random.fold_in(key, 6), position), (shards_of,), jnp.float32, smallest / len(split), high / len(split))
        return jnp.repeat(jnp.exp(steps), shape[position] // shards_of).reshape((-1,) + (1,) * (len(shape) - position - 1))

    level = one(*split[0])
    for cut in split[1:]:
        level = level * one(*cut)
    return level


def bell_draw(stream_key, extent, deviation, most, cuts=(), held_as=jnp.bfloat16):
    result = jax.random.normal(stream_key, extent, jnp.float32) * deviation
    if len(cuts) > 0:
        result = block_scale(stream_key, extent, cuts, -0.22, 0.18) * result
    return jnp.clip(result, min=-most, max=most).astype(held_as)


def setup_inputs(seed: int = 0) -> dict:
    seeds = jax.random.split(jax.random.key(seed), 4)
    return {
        "momentum": bell_draw(seeds[0], (EXPERTS, ROWS, COLS), 1.0, 6.0, ((1, 32), (2, 8)), jnp.float32),
        "gradient": bell_draw(seeds[1], (EXPERTS, ROWS, COLS), 1.0, 6.0, ((1, 32), (2, 8))),
        "basis_in": bell_draw(seeds[2], (EXPERTS, COLS, RANK), COLS ** -0.5, 0.125, ((1, 8),)),
    }


def expert_step(pieces):
    momentum, gradient, basis_in = pieces
    buffer = momentum + gradient.astype(jnp.float32)
    buffer_half = buffer.astype(jnp.bfloat16)
    projected = jnp.dot(buffer_half.astype(jnp.float32), basis_in.astype(jnp.float32), preferred_element_type=jnp.float32)
    gram_full = jnp.dot(projected.T, projected, precision=lax.Precision.HIGHEST)
    factor = jnp.linalg.cholesky(gram_full)
    orthonormal = lax.linalg.triangular_solve(factor, projected, left_side=False, lower=True, transpose_a=True).astype(jnp.bfloat16)
    reduced = jnp.dot(buffer_half.T.astype(jnp.float32), orthonormal.astype(jnp.float32), preferred_element_type=jnp.float32)
    momentum_new = buffer - 0.1 * jnp.dot(orthonormal.astype(jnp.float32), reduced.T, precision=lax.Precision.HIGHEST)
    squares = lax.optimization_barrier(jnp.sum(reduced * reduced, axis=0, keepdims=True))
    new_basis = (reduced * lax.rsqrt(squares + 1e-06)).astype(jnp.bfloat16)
    update_scale = math.sqrt(ROWS * COLS / RANK)
    direction = (update_scale * jnp.dot(orthonormal.astype(jnp.float32), new_basis.T.astype(jnp.float32), preferred_element_type=jnp.float32)).astype(jnp.bfloat16)
    return (momentum_new, direction)

def reference(momentum, gradient, basis_in):
    momentum_new, direction = lax.map(expert_step, (momentum, gradient, basis_in))
    return (momentum_new, direction)
```

```python
import math

import jax
import jax.numpy as jnp
from jax import lax
from jax.experimental import pallas as pl
from jax.experimental.pallas import tpu as pltpu
from jax.sharding import PartitionSpec as P

ROWS = 7168
COLS = 2048
RANK = 512
EXPERTS = 2
BLOCK = 128
PANEL = 8
BLOCKS = RANK // BLOCK
PANELS = BLOCK // PANEL
HIGHEST = lax.Precision.HIGHEST


def lanes_of(value, lane):
    return jnp.broadcast_to(value[:, lane : lane + 1], (PANEL, BLOCK))


def row_of(value, row):
    return jnp.broadcast_to(value[row : row + 1, :], (PANEL, BLOCK))


def small_inverse(panel, base, row):
    cols = [lanes_of(panel, base + j) for j in range(PANEL)]
    snap = [jnp.zeros((PANEL, BLOCK), jnp.float32) for _ in range(PANEL)]
    roots = jnp.zeros((PANEL, BLOCK), jnp.float32)
    for j in range(PANEL):
        here = row == j
        root = lax.rsqrt(row_of(cols[j], j))
        inv = root * root
        roots = jnp.where(here, root, roots)
        pivot = cols[j]
        for k in range(PANEL):
            if k == j:
                continue
            entry = row_of(cols[k], j)
            if k < j:
                snap[k] = jnp.where(here, entry, snap[k])
            scaled = entry * inv
            cols[k] = jnp.where(here, scaled, cols[k] - pivot * scaled)
        cols[j] = jnp.where(here, inv, -(pivot * inv))
        snap[j] = jnp.where(here, 1.0, snap[j])
    return cols, [roots * s for s in snap]


def combine(cols, value):
    terms = [cols[j] * row_of(value, j) for j in range(PANEL)]
    while len(terms) > 1:
        terms = [terms[i] + terms[i + 1] for i in range(0, len(terms), 2)]
    return terms[0]


def block_inverse_factor(groups):
    row = lax.broadcasted_iota(jnp.int32, (PANEL, BLOCK), 0)
    lane = lax.broadcasted_iota(jnp.int32, (PANEL, BLOCK), 1)
    for k in range(PANELS):
        base = k * PANEL
        inside = (lane >= base) & (lane < base + PANEL)
        unit = (lane == row + base).astype(jnp.float32)
        for e in range(EXPERTS):
            panel = groups[e][k]
            full, factor = small_inverse(panel, base, row)
            panel = jnp.where(inside, unit, panel)
            groups[e][k] = combine(factor, panel)
            if k + 1 < PANELS:
                solved = combine(full, panel)
                rows = [row_of(solved, j) for j in range(PANEL)]
                for i in range(k + 1, PANELS):
                    old = groups[e][i]
                    terms = [lanes_of(old, base + j) * rows[j] for j in range(PANEL)]
                    while len(terms) > 1:
                        terms = [terms[t] + terms[t + 1] for t in range(0, len(terms), 2)]
                    groups[e][i] = jnp.where(inside, 0.0, old) - terms[0]
    return groups


def factor_kernel(gram_ref, out_ref, work_ref):
    for e in range(EXPERTS):
        for i in range(BLOCKS):
            work_ref[e, i] = gram_ref[e, i * BLOCK : (i + 1) * BLOCK, :]
    big_row = lax.broadcasted_iota(jnp.int32, (BLOCK, BLOCK), 0)
    big_lane = lax.broadcasted_iota(jnp.int32, (BLOCK, BLOCK), 1)
    wide = lax.broadcasted_iota(jnp.int32, (BLOCK, RANK), 1)

    def step(k, carry):
        at = pl.multiple_of(k * BLOCK, BLOCK)
        groups = []
        for e in range(EXPERTS):
            groups.append(
                [work_ref[e, k, i * PANEL : (i + 1) * PANEL, pl.ds(at, BLOCK)] for i in range(PANELS)]
            )
        groups = block_inverse_factor(groups)
        own = (wide >= at) & (wide < at + BLOCK)
        for e in range(EXPERTS):
            inverse = jnp.where(big_row >= big_lane, jnp.concatenate(groups[e], axis=0), 0.0)
            work_ref[e, k] = jnp.dot(
                inverse, work_ref[e, k], precision=HIGHEST, preferred_element_type=jnp.float32
            )
            work_ref[e, k, :, pl.ds(at, BLOCK)] = inverse
        for i in range(1, BLOCKS):

            @pl.when(i > k)
            def _():
                for e in range(EXPERTS):
                    left = work_ref[e, k, :, i * BLOCK : (i + 1) * BLOCK].T
                    change = jnp.dot(
                        left, work_ref[e, k], precision=HIGHEST, preferred_element_type=jnp.float32
                    )
                    work_ref[e, i] = jnp.where(own, 0.0, work_ref[e, i]) - change

        return carry

    lax.fori_loop(0, BLOCKS, step, 0)
    for e in range(EXPERTS):
        for i in range(BLOCKS):
            row = lax.broadcasted_iota(jnp.int32, (BLOCK, RANK), 0) + i * BLOCK
            out_ref[e, i * BLOCK : (i + 1) * BLOCK, :] = jnp.where(row >= wide, work_ref[e, i], 0.0)


def inverse_factor(gram):
    return pl.pallas_call(
        factor_kernel,
        out_shape=jax.ShapeDtypeStruct(gram.shape, jnp.float32),
        in_specs=[pl.BlockSpec(memory_space=pltpu.VMEM)],
        out_specs=pl.BlockSpec(memory_space=pltpu.VMEM),
        scratch_shapes=[pltpu.VMEM((EXPERTS, BLOCKS, BLOCK, RANK), jnp.float32)],
        compiler_params=pltpu.CompilerParams(vmem_limit_bytes=24 * 1024 * 1024),
    )(gram)


def spread(chunks, axis):
    return lax.all_to_all(chunks, axis, split_axis=0, concat_axis=0, tiled=True)


def share(value, axis, count):
    return spread(jnp.broadcast_to(value[None], (count,) + value.shape), axis)


def split_halves(value):
    high = value.astype(jnp.bfloat16)
    low = (value - high.astype(jnp.float32)).astype(jnp.bfloat16)
    return high, low


def make_local(row_count, col_count):
    def local(momentum, gradient, basis_in):
        experts, rows, cols = momentum.shape
        rank = basis_in.shape[-1]
        buffer = momentum + gradient.astype(jnp.float32)
        half = buffer.astype(jnp.bfloat16)
        partial = jnp.einsum("erc,eck->erk", half, basis_in, preferred_element_type=jnp.float32)
        piece = partial.astype(jnp.bfloat16).reshape(col_count, experts * rows // col_count, rank)
        mine = jnp.sum(spread(piece, "col").astype(jnp.float32), axis=0).astype(jnp.bfloat16)
        projected = share(mine, "col", col_count).reshape(experts, rows, rank)

        col = lax.axis_index("col")
        slabs = col_count // experts
        width = rank // slabs
        one = lax.dynamic_index_in_dim(projected, col % experts, 0, keepdims=False)
        slab = lax.dynamic_slice_in_dim(one, (col // experts) * width, width, axis=1)
        gram_partial = jnp.einsum("rk,rl->kl", slab, one, preferred_element_type=jnp.float32)
        wide_partial = jnp.einsum(
            "erc,erk->eck", half, projected, preferred_element_type=jnp.float32
        ).astype(jnp.bfloat16)
        gram_high, gram_low = split_halves(gram_partial.reshape(row_count, width // row_count, rank))
        wide_rows = experts * cols // row_count
        packed = jnp.concatenate(
            [wide_partial.reshape(row_count, wide_rows, rank), gram_high, gram_low], axis=1
        )
        arrived = spread(packed, "row").astype(jnp.float32)
        gram_rows = width // row_count
        wide_mine = jnp.sum(arrived[:, :wide_rows], axis=0).astype(jnp.bfloat16)
        gram_mine = jnp.sum(
            arrived[:, wide_rows : wide_rows + gram_rows] + arrived[:, wide_rows + gram_rows :], axis=0
        )
        gram_slab = share(gram_mine, "row", row_count).reshape(width, rank)
        wide = share(wide_mine, "row", row_count).reshape(experts, cols, rank)
        gram = share(gram_slab, "col", col_count).reshape(slabs, experts, width, rank)
        gram = jnp.swapaxes(gram, 0, 1).reshape(experts, rank, rank)

        inverse = inverse_factor(gram)
        inv_high, inv_low = split_halves(inverse)

        def solve(value):
            return jnp.einsum(
                "erk,elk->erl", value, inv_high, preferred_element_type=jnp.float32
            ) + jnp.einsum("erk,elk->erl", value, inv_low, preferred_element_type=jnp.float32)

        reduced = solve(wide)
        squares = jnp.sum(reduced * reduced, axis=1)
        squares = jnp.sum(share(squares, "col", col_count), axis=0)[:, None, :]
        orthonormal = solve(projected).astype(jnp.bfloat16)
        new_basis = (reduced * lax.rsqrt(squares + 1e-06)).astype(jnp.bfloat16)
        momentum_new = buffer - 0.1 * jnp.einsum(
            "erk,eck->erc",
            orthonormal,
            reduced.astype(jnp.bfloat16),
            preferred_element_type=jnp.float32,
        )
        update_scale = math.sqrt(ROWS * COLS / RANK)
        direction = (
            update_scale
            * jnp.einsum(
                "erk,eck->erc", orthonormal, new_basis, preferred_element_type=jnp.float32
            )
        ).astype(jnp.bfloat16)
        return (momentum_new, direction)

    return local


def solution(mesh):
    placed = (P(None, "row", "col"), P(None, "row", "col"), P(None, "col", None))
    return jax.shard_map(
        make_local(mesh.shape["row"], mesh.shape["col"]),
        mesh=mesh,
        in_specs=placed,
        out_specs=(P(None, "row", "col"), P(None, "row", "col")),
        check_vma=False,
    )
```

```python
import math

import jax
import jax.numpy as jnp
import numpy as np
from jax import lax
from jax.experimental import pallas as pl
from jax.experimental.pallas import tpu as pltpu
from jax.sharding import PartitionSpec as P

ROWS = 7168
COLS = 2048
RANK = 512
BLOCK = 128
PANEL = 8
BLOCKS = RANK // BLOCK
PANELS = BLOCK // PANEL
KEPT = 3
X_SIZE = 4
Z_SIZE = 8


def lanes_of(value, lane):
    return jnp.broadcast_to(value[:, lane : lane + 1], (PANEL, BLOCK))


def row_of(value, row):
    return jnp.broadcast_to(value[row : row + 1, :], (PANEL, BLOCK))


def added(terms):
    while len(terms) > 1:
        terms = [terms[i] + terms[i + 1] for i in range(0, len(terms), 2)]
    return terms[0]


def small_inverse(cols, row):
    cols = list(cols)
    factor = [jnp.zeros((PANEL, BLOCK), jnp.float32) for _ in range(PANEL)]
    for j in range(0, PANEL, 2):
        first, second = row == j, row == j + 1
        both = first | second
        left, right = cols[j], cols[j + 1]
        a, b, c = row_of(left, j), row_of(right, j), row_of(right, j + 1)
        root = lax.rsqrt(a * c - b * b)
        inv = root * root
        ia, ib, ic = c * inv, -(b * inv), a * inv
        root_a = lax.rsqrt(a)
        ratio = b * (root_a * root_a)
        root_c = lax.rsqrt(c - b * ratio)
        left_m = jnp.where(first, -1.0, jnp.where(second, 0.0, left))
        right_m = jnp.where(first, 0.0, jnp.where(second, -1.0, right))
        for k in range(PANEL):
            if k in (j, j + 1):
                continue
            top, low = row_of(cols[k], j), row_of(cols[k], j + 1)
            rest = jnp.where(both, 0.0, cols[k])
            cols[k] = rest - (left_m * (ia * top + ib * low) + right_m * (ib * top + ic * low))
            if k < j:
                factor[k] = jnp.where(
                    first, top * root_a, jnp.where(second, (low - ratio * top) * root_c, factor[k])
                )
        factor[j] = jnp.where(first, root_a, jnp.where(second, -(ratio * root_c), factor[j]))
        factor[j + 1] = jnp.where(second, root_c, factor[j + 1])
        cols[j] = -(left_m * ia + right_m * ib)
        cols[j + 1] = -(left_m * ib + right_m * ic)
    return cols, factor


def combine(cols, value):
    return added([cols[j] * row_of(value, j) for j in range(PANEL)])


def block_inverse_factor(groups):
    row = lax.broadcasted_iota(jnp.int32, (PANEL, BLOCK), 0)
    lane = lax.broadcasted_iota(jnp.int32, (PANEL, BLOCK), 1)
    block = [lanes_of(groups[0], j) for j in range(PANEL)]
    for k in range(PANELS):
        base = k * PANEL
        inside = (lane >= base) & (lane < base + PANEL)
        full, factor = small_inverse(block, row)
        panel = jnp.where(inside, (lane == row + base).astype(jnp.float32), groups[k])
        if k + 1 < PANELS:
            down = [lanes_of(groups[k + 1], base + j) for j in range(PANEL)]
            block = []
            for m in range(base + PANEL, base + 2 * PANEL):
                column = combine(full, lanes_of(groups[k], m))
                block.append(lanes_of(groups[k + 1], m) - combine(down, column))
            solved = combine(full, panel)
            rows = [row_of(solved, j) for j in range(PANEL)]
            for i in range(k + 1, PANELS):
                old = groups[i]
                change = added([lanes_of(old, base + j) * rows[j] for j in range(PANEL)])
                groups[i] = jnp.where(inside, 0.0, old) - change
        groups[k] = jnp.where(lane <= row + base, combine(factor, panel), 0.0)
    return groups


def split_halves(value):
    high = value.astype(jnp.bfloat16)
    low = (value - high.astype(jnp.float32)).astype(jnp.bfloat16)
    return high, low


def product(left, right, left_axis):
    return lax.dot_general(
        jnp.concatenate([left[0], left[0], left[1]], axis=left_axis),
        jnp.concatenate([right[0], right[1], right[0]], axis=0),
        (((left_axis,), (0,)), ((), ())),
        preferred_element_type=jnp.float32,
    )


def factor_kernel(where_ref, own_ref, one_ref, two_ref, three_ref, out_ref, slab_ref, work_ref):
    here = where_ref[0]
    for back, ref in enumerate((own_ref, one_ref, two_ref, three_ref)):
        slab_ref[lax.rem(here + (BLOCKS - back), BLOCKS)] = ref[...]

    def block(i, j):
        if j - i < KEPT:
            return slab_ref[i, :, (j - i) * BLOCK : (j - i + 1) * BLOCK]
        return slab_ref[j, :, (BLOCKS + i - j) * BLOCK : (BLOCKS + i - j + 1) * BLOCK].T

    most = jnp.maximum(
        jnp.maximum(block(0, 0), block(1, 1)), jnp.maximum(block(2, 2), block(3, 3))
    )
    most = jnp.max(jnp.max(most, axis=0, keepdims=True), axis=1, keepdims=True)
    scale = 1.0 / most
    for i in range(BLOCKS):
        for j in range(i, BLOCKS):
            work_ref[i, :, j * BLOCK : (j + 1) * BLOCK] = block(i, j) * scale
    back_scale = lax.rsqrt(most)

    for k in range(BLOCKS):
        at, to = k * BLOCK, (k + 1) * BLOCK
        groups = [work_ref[k, i * PANEL : (i + 1) * PANEL, at:to] for i in range(PANELS)]
        inverse = jnp.concatenate(block_inverse_factor(groups), axis=0)
        work_ref[k, :, at:to] = inverse
        pair = split_halves(inverse)
        if k > 0:
            work_ref[k, :, :at] = product(pair, split_halves(work_ref[k, :, :at]), 1)
        if k + 1 < BLOCKS:
            upper = product(pair, split_halves(work_ref[k, :, to:]), 1)
            work_ref[k, :, to:] = upper
            upper = split_halves(upper)
            whole = split_halves(work_ref[k])
            for i in range(k + 1, BLOCKS):
                left = tuple(part[:, (i - k - 1) * BLOCK : (i - k) * BLOCK] for part in upper)
                work_ref[i, :, i * BLOCK :] -= product(
                    left, tuple(part[:, i * BLOCK :] for part in whole), 0
                )
                change = product(left, tuple(part[:, :to] for part in whole), 0)
                if k > 0:
                    work_ref[i, :, :at] -= change[:, :at]
                work_ref[i, :, at:to] = -change[:, at:]
    for i in range(BLOCKS):
        to = (i + 1) * BLOCK
        rows = slice(i * BLOCK, to)
        out_ref[rows, :to] = (work_ref[i, :, :to] * back_scale).astype(jnp.bfloat16)
        if to < RANK:
            out_ref[rows, to:] = jnp.zeros((BLOCK, RANK - to), jnp.bfloat16)


def inverse_factor(where, slabs):
    vmem = pl.BlockSpec(memory_space=pltpu.VMEM)
    return pl.pallas_call(
        factor_kernel,
        out_shape=jax.ShapeDtypeStruct((RANK, RANK), jnp.bfloat16),
        in_specs=[pl.BlockSpec(memory_space=pltpu.SMEM)] + [vmem] * BLOCKS,
        out_specs=vmem,
        scratch_shapes=[
            pltpu.VMEM((BLOCKS, BLOCK, KEPT * BLOCK), jnp.float32),
            pltpu.VMEM((BLOCKS, BLOCK, RANK), jnp.float32),
        ],
        compiler_params=pltpu.CompilerParams(vmem_limit_bytes=24 * 1024 * 1024),
        cost_estimate=pl.CostEstimate(flops=2 * 10**10, bytes_accessed=0, transcendentals=0),
    )(where, *slabs)


def sum_kernel(*refs):
    refs[-1][...] = added([ref[...] for ref in refs[:-2]])


def summed(terms, after):
    vmem = pl.BlockSpec(memory_space=pltpu.VMEM)
    return pl.pallas_call(
        sum_kernel,
        out_shape=jax.ShapeDtypeStruct(terms[0].shape, terms[0].dtype),
        in_specs=[vmem] * len(terms) + [pl.BlockSpec(memory_space=pl.ANY)],
        out_specs=vmem,
    )(*terms, after)


def spread(chunks, axis):
    return lax.all_to_all(chunks, axis, split_axis=0, concat_axis=0, tiled=True)


def share(value, axis, count):
    return spread(jnp.broadcast_to(value[None], (count,) + value.shape), axis)


def swap(value, axis, count, mask):
    return lax.ppermute(value, axis, [(i, i ^ mask) for i in range(count)])


def pick(first, value, other):
    return jnp.stack([jnp.where(first, value, other), jnp.where(first, other, value)])


def make_local(row_count, col_count):
    def bit(index, mask):
        return lax.convert_element_type(lax.bitwise_and(index, np.uint32(mask)) != 0, jnp.uint32)

    def item(stack, index):
        return lax.dynamic_index_in_dim(stack, index, 0, keepdims=False)

    def quad(value, axis, count, low):
        return [value] + [swap(value, axis, count, step * low) for step in (1, 2, 3)]

    def row_sum(value, row, after):
        pieces = value.reshape(X_SIZE, value.shape[0] // X_SIZE, value.shape[1])
        plane = lax.div(row, np.uint32(Z_SIZE))
        terms = [item(pieces, plane)]
        for step in range(1, X_SIZE):
            send = item(pieces, lax.bitwise_xor(plane, np.uint32(step)))
            terms.append(swap(send, "row", row_count, step * Z_SIZE))
        value = added(terms)
        value = value + swap(value, "row", row_count, 4)
        value = summed(quad(value, "row", row_count, 1), after)
        parts = quad(value, "row", row_count, Z_SIZE)
        low = bit(plane, 1) == 0
        both = pick(bit(plane, 2) == 0, pick(low, parts[0], parts[1]), pick(low, parts[2], parts[3]))
        return both.reshape(X_SIZE * value.shape[0], value.shape[1])

    def local(momentum, gradient, basis_in):
        experts, rows, cols = momentum.shape
        rank = basis_in.shape[-1]
        row = lax.axis_index("row").astype(jnp.uint32)
        col = lax.axis_index("col").astype(jnp.uint32)
        expert = lax.rem(col, np.uint32(experts))
        place = lax.div(col, np.uint32(experts))
        first = expert == 0
        buffer = momentum + gradient.astype(jnp.float32)
        half = buffer.astype(jnp.bfloat16)
        partial = jnp.einsum(
            "erc,eck->erk", half, basis_in, preferred_element_type=jnp.float32
        ).astype(jnp.bfloat16)
        term = item(partial, expert) + swap(item(partial, 1 - expert), "col", col_count, 1)
        terms = [part.astype(jnp.float32) for part in quad(term, "col", col_count, experts)]
        projected = added(terms).astype(jnp.bfloat16)

        turned = lax.dynamic_slice_in_dim(
            jnp.concatenate([projected, projected[:, : (KEPT - 1) * BLOCK]], axis=1),
            place * np.uint32(BLOCK),
            KEPT * BLOCK,
            axis=1,
        )
        whole = jnp.stack(
            [item(half, expert), swap(item(half, 1 - expert), "col", col_count, 1)]
        )
        wide = jnp.einsum("hrc,rk->hck", whole, projected, preferred_element_type=jnp.float32)
        wide = wide.astype(jnp.bfloat16).reshape(row_count, 2 * cols // row_count, rank)
        wide = jnp.sum(spread(wide, "row").astype(jnp.float32), axis=0).astype(jnp.bfloat16)

        slab = row_sum(
            jnp.einsum("rk,rl->kl", turned[:, :BLOCK], turned, preferred_element_type=jnp.float32), row, wide
        )
        slabs = [slab]
        for step in range(1, BLOCKS):
            turn = [(i, (i + step * experts) % col_count) for i in range(col_count)]
            slabs.append(lax.ppermute(slab, "col", turn))
        wide = share(wide, "row", row_count).reshape(2 * cols, rank)

        inverse = inverse_factor(jnp.reshape(place, (1,)).astype(jnp.int32), slabs)

        def solve(value):
            return jnp.einsum("rk,lk->rl", value, inverse, preferred_element_type=jnp.float32)

        reduced = solve(wide)
        squares = jnp.sum(reduced * reduced, axis=0, keepdims=True)
        squares = added(quad(squares, "col", col_count, experts))
        orthonormal = solve(projected).astype(jnp.bfloat16)

        def outer(right):
            value = jnp.einsum("rk,ck->rc", orthonormal, right, preferred_element_type=jnp.float32)
            return value[:, :cols], value[:, cols:]

        own, other = outer(reduced.astype(jnp.bfloat16))
        other = swap((0.1 * other).astype(jnp.bfloat16), "col", col_count, 1)
        momentum_new = buffer - pick(first, 0.1 * own, other.astype(jnp.float32))
        new_basis = (reduced * lax.rsqrt(squares + 1e-06)).astype(jnp.bfloat16)
        update_scale = math.sqrt(ROWS * COLS / RANK)
        own, other = outer(new_basis)
        own = (update_scale * own).astype(jnp.bfloat16)
        other = swap((update_scale * other).astype(jnp.bfloat16), "col", col_count, 1)
        return (momentum_new, pick(first, own, other))

    return local


def solution(mesh):
    placed = (P(None, "row", "col"), P(None, "row", "col"), P(None, "col", None))
    return jax.shard_map(
        make_local(mesh.shape["row"], mesh.shape["col"]),
        mesh=mesh,
        in_specs=placed,
        out_specs=(P(None, "row", "col"), P(None, "row", "col")),
        check_vma=False,
    )
```

```python
import functools
import math

import jax
import jax.numpy as jnp
import numpy as np
from jax import lax
from jax.experimental import pallas as pl
from jax.experimental.pallas import tpu as pltpu
from jax.sharding import PartitionSpec as P

ROWS = 7168
COLS = 2048
RANK = 512
BLOCK = 128
PANEL = 8
BLOCKS = RANK // BLOCK
PANELS = BLOCK // PANEL
KEPT = 3
X_SIZE = 4
Z_SIZE = 8


def lanes_of(value, lane):
    return jnp.broadcast_to(value[:, lane : lane + 1], (PANEL, BLOCK))


def row_of(value, row):
    return jnp.broadcast_to(value[row : row + 1, :], (PANEL, BLOCK))


def added(terms):
    while len(terms) > 1:
        terms = [terms[i] + terms[i + 1] for i in range(0, len(terms), 2)]
    return terms[0]


def small_inverse(cols, row):
    cols = list(cols)
    factor = [jnp.zeros((PANEL, BLOCK), jnp.float32) for _ in range(PANEL)]
    for j in range(0, PANEL, 2):
        first, second = row == j, row == j + 1
        both = first | second
        left, right = cols[j], cols[j + 1]
        a, b, c = row_of(left, j), row_of(right, j), row_of(right, j + 1)
        root = lax.rsqrt(a * c - b * b)
        inv = root * root
        root_a = lax.rsqrt(a)
        ratio = b * (root_a * root_a)
        root_c = lax.rsqrt(c - b * ratio)
        left_m = jnp.where(first, -1.0, jnp.where(second, 0.0, left))
        right_m = jnp.where(first, 0.0, jnp.where(second, -1.0, right))
        for k in range(PANEL):
            if k in (j, j + 1):
                continue
            top, low = row_of(cols[k], j), row_of(cols[k], j + 1)
            rest = jnp.where(both, 0.0, cols[k])
            cols[k] = rest - inv * (left_m * (c * top - b * low) + right_m * (a * low - b * top))
            if k < j:
                factor[k] = jnp.where(
                    first, top * root_a, jnp.where(second, (low - ratio * top) * root_c, factor[k])
                )
        factor[j] = jnp.where(first, root_a, jnp.where(second, -(ratio * root_c), factor[j]))
        factor[j + 1] = jnp.where(second, root_c, factor[j + 1])
        cols[j] = inv * (right_m * b - left_m * c)
        cols[j + 1] = inv * (left_m * b - right_m * a)
    return cols, factor


def combine(cols, value):
    return added([cols[j] * row_of(value, j) for j in range(PANEL)])


def block_inverse_factor(groups, tasks):
    row = lax.broadcasted_iota(jnp.int32, (PANEL, BLOCK), 0)
    lane = lax.broadcasted_iota(jnp.int32, (PANEL, BLOCK), 1)
    block = [lanes_of(groups[0], j) for j in range(PANEL)]
    for k in range(PANELS):
        base = k * PANEL
        inside = (lane >= base) & (lane < base + PANEL)
        full, factor = small_inverse(block, row)
        panel = jnp.where(inside, (lane == row + base).astype(jnp.float32), groups[k])
        if k + 1 < PANELS:
            down = [lanes_of(groups[k + 1], base + j) for j in range(PANEL)]
            block = []
            for m in range(base + PANEL, base + 2 * PANEL):
                column = combine(full, lanes_of(groups[k], m))
                block.append(lanes_of(groups[k + 1], m) - combine(down, column))
            solved = combine(full, panel)
            rows = [row_of(solved, j) for j in range(PANEL)]
            for i in range(k + 1, PANELS):
                old = groups[i]
                change = added([lanes_of(old, base + j) * rows[j] for j in range(PANEL)])
                groups[i] = jnp.where(inside, 0.0, old) - change
        groups[k] = jnp.where(lane <= row + base, combine(factor, panel), 0.0)
        if k < len(tasks):
            tasks[k]()
    return groups


def split_halves(value):
    high = value.astype(jnp.bfloat16)
    low = (value - high.astype(jnp.float32)).astype(jnp.bfloat16)
    return high, low


def wide_terms(value):
    high, low = split_halves(value)
    return jnp.concatenate([high, high, low], axis=1)


def product(terms, right):
    high, low = split_halves(right)
    return jnp.dot(
        terms, jnp.concatenate([high, low, high], axis=0), preferred_element_type=jnp.float32
    )


def later_products(work_ref, k, inverse, columns):
    before, through = slice(0, k * BLOCK), slice(0, (k + 1) * BLOCK)
    lefts = {}

    def solve(j):
        upper = product(inverse, work_ref[k, :, columns(j)])
        work_ref[k, :, columns(j)] = upper
        lefts[j] = wide_terms(upper.T)

    def solve_before():
        work_ref[k, :, before] = product(inverse, work_ref[k, :, before])

    def update(i, j):
        work_ref[i, :, columns(j)] -= product(lefts[i], work_ref[k, :, columns(j)])

    def update_before(i):
        change = product(lefts[i], work_ref[k, :, through])
        if k > 0:
            work_ref[i, :, before] -= change[:, before]
        work_ref[i, :, columns(k)] = -change[:, columns(k)]

    rest = range(k + 1, BLOCKS)
    tasks = [functools.partial(solve, j) for j in rest[1:]]
    if k > 0:
        tasks.append(solve_before)
    for i in rest:
        tasks += [functools.partial(update, i, j) for j in range(i, BLOCKS) if j > k + 1]
        tasks.append(functools.partial(update_before, i))
    if k + 1 < BLOCKS:
        solve(k + 1)
        update(k + 1, k + 1)
        return tasks
    for task in tasks:
        task()
    return []


def factor_kernel(where_ref, own_ref, one_ref, two_ref, three_ref, out_ref, slab_ref, work_ref):
    here = where_ref[0]
    for back, ref in enumerate((own_ref, one_ref, two_ref, three_ref)):
        slab_ref[lax.rem(here + (BLOCKS - back), BLOCKS)] = ref[...]

    def block(i, j):
        if j - i < KEPT:
            return slab_ref[i, :, (j - i) * BLOCK : (j - i + 1) * BLOCK]
        return slab_ref[j, :, (BLOCKS + i - j) * BLOCK : (BLOCKS + i - j + 1) * BLOCK].T

    most = jnp.maximum(
        jnp.maximum(block(0, 0), block(1, 1)), jnp.maximum(block(2, 2), block(3, 3))
    )
    most = jnp.max(jnp.max(most, axis=0, keepdims=True), axis=1, keepdims=True)
    scale = 1.0 / most
    for i in range(BLOCKS):
        for j in range(i, BLOCKS):
            work_ref[i, :, j * BLOCK : (j + 1) * BLOCK] = block(i, j) * scale
    back_scale = lax.rsqrt(most)

    def columns(j):
        return slice(j * BLOCK, (j + 1) * BLOCK)

    tasks = []
    for k in range(BLOCKS):
        at, to = k * BLOCK, (k + 1) * BLOCK
        groups = [work_ref[k, i * PANEL : (i + 1) * PANEL, at:to] for i in range(PANELS)]
        inverse = jnp.concatenate(block_inverse_factor(groups, tasks), axis=0)
        work_ref[k, :, at:to] = inverse
        tasks = later_products(work_ref, k, wide_terms(inverse), columns)
    for i in range(BLOCKS):
        to = (i + 1) * BLOCK
        rows = slice(i * BLOCK, to)
        out_ref[rows, :to] = (work_ref[i, :, :to] * back_scale).astype(jnp.bfloat16)
        if to < RANK:
            out_ref[rows, to:] = jnp.zeros((BLOCK, RANK - to), jnp.bfloat16)


def inverse_factor(where, slabs):
    vmem = pl.BlockSpec(memory_space=pltpu.VMEM)
    return pl.pallas_call(
        factor_kernel,
        out_shape=jax.ShapeDtypeStruct((RANK, RANK), jnp.bfloat16),
        in_specs=[pl.BlockSpec(memory_space=pltpu.SMEM)] + [vmem] * BLOCKS,
        out_specs=vmem,
        scratch_shapes=[
            pltpu.VMEM((BLOCKS, BLOCK, KEPT * BLOCK), jnp.float32),
            pltpu.VMEM((BLOCKS, BLOCK, RANK), jnp.float32),
        ],
        compiler_params=pltpu.CompilerParams(vmem_limit_bytes=24 * 1024 * 1024),
        cost_estimate=pl.CostEstimate(flops=2 * 10**10, bytes_accessed=0, transcendentals=0),
    )(where, *slabs)


def place_kernel(where_ref, *refs):
    parts, out_ref = refs[:X_SIZE], refs[-1]
    for step, ref in enumerate(parts):
        out_ref[lax.bitwise_xor(where_ref[0], step)] = ref[...]


def placed_parts(where, parts, after):
    vmem = pl.BlockSpec(memory_space=pltpu.VMEM)
    return pl.pallas_call(
        place_kernel,
        out_shape=jax.ShapeDtypeStruct((X_SIZE,) + parts[0].shape, parts[0].dtype),
        in_specs=[pl.BlockSpec(memory_space=pltpu.SMEM)] + [vmem] * (X_SIZE + 1),
        out_specs=vmem,
    )(where, *parts, after)


def wide_kernel(own_ref, other_ref, right_ref, _, out_ref):
    for i, ref in enumerate((own_ref, other_ref)):
        out_ref[i] = lax.dot_general(
            ref[...], right_ref[...], (((0,), (0,)), ((), ())), preferred_element_type=jnp.float32
        ).astype(out_ref.dtype)


def wide_product(own, other, right, after):
    vmem = pl.BlockSpec(memory_space=pltpu.VMEM)
    return pl.pallas_call(
        wide_kernel,
        out_shape=jax.ShapeDtypeStruct((2, own.shape[1], right.shape[1]), jnp.bfloat16),
        in_specs=[vmem] * 4,
        out_specs=vmem,
        compiler_params=pltpu.CompilerParams(vmem_limit_bytes=24 * 1024 * 1024),
    )(own, other, right, after)


def spread(chunks, axis):
    return lax.all_to_all(chunks, axis, split_axis=0, concat_axis=0, tiled=True)


def share(value, axis, count):
    return spread(jnp.broadcast_to(value[None], (count,) + value.shape), axis)


def swap(value, axis, count, mask):
    return lax.ppermute(value, axis, [(i, i ^ mask) for i in range(count)])


def pick(first, value, other):
    return jnp.stack([jnp.where(first, value, other), jnp.where(first, other, value)])


def make_local(row_count, col_count):
    def item(stack, index):
        return lax.dynamic_index_in_dim(stack, index, 0, keepdims=False)

    def quad(value, axis, count, low):
        return [value] + [swap(value, axis, count, step * low) for step in (1, 2, 3)]

    def x_sum(value, plane):
        pieces = value.reshape(X_SIZE, value.shape[0] // X_SIZE, value.shape[1])
        terms = [item(pieces, plane)]
        for step in range(1, X_SIZE):
            send = item(pieces, lax.bitwise_xor(plane, np.uint32(step)))
            terms.append(swap(send, "row", row_count, step * Z_SIZE))
        return added(terms)

    def z_sum(value):
        value = value + swap(value, "row", row_count, 4)
        return added(quad(value, "row", row_count, 1))

    def local(momentum, gradient, basis_in):
        experts, rows, cols = momentum.shape
        rank = basis_in.shape[-1]
        row = lax.axis_index("row").astype(jnp.uint32)
        col = lax.axis_index("col").astype(jnp.uint32)
        expert = lax.rem(col, np.uint32(experts))
        place = lax.div(col, np.uint32(experts))
        first = expert == 0
        buffer = lax.optimization_barrier(momentum + gradient.astype(jnp.float32))
        half = buffer.astype(jnp.bfloat16)
        partial = jnp.einsum(
            "erc,eck->erk", half, basis_in, preferred_element_type=jnp.float32
        ).astype(jnp.bfloat16)
        term = item(partial, expert) + swap(item(partial, 1 - expert), "col", col_count, 1)
        terms = [part.astype(jnp.float32) for part in quad(term, "col", col_count, experts)]
        projected = added(terms).astype(jnp.bfloat16)

        turned = lax.dynamic_slice_in_dim(
            jnp.concatenate([projected, projected[:, : (KEPT - 1) * BLOCK]], axis=1),
            place * np.uint32(BLOCK),
            KEPT * BLOCK,
            axis=1,
        )
        gram = jnp.einsum("rk,rl->kl", turned[:, :BLOCK], turned, preferred_element_type=jnp.float32)
        plane = lax.div(row, np.uint32(Z_SIZE))
        gram = x_sum(gram, plane)
        left = swap(item(half, 1 - expert), "col", col_count, 1)
        wide = wide_product(item(half, expert), left, projected, gram[:PANEL, :BLOCK])
        wide = wide.reshape(row_count, 2 * cols // row_count, rank)
        wide = jnp.sum(spread(wide, "row").astype(jnp.float32), axis=0).astype(jnp.bfloat16)
        gram = z_sum(gram)
        slab = placed_parts(
            jnp.reshape(plane, (1,)).astype(jnp.int32),
            quad(gram, "row", row_count, Z_SIZE),
            wide[: 2 * PANEL, :BLOCK],
        ).reshape(BLOCK, KEPT * BLOCK)
        slabs = [slab]
        for step in range(1, BLOCKS):
            turn = [(i, (i + step * experts) % col_count) for i in range(col_count)]
            slabs.append(lax.ppermute(slab, "col", turn))
        wide = share(wide, "row", row_count).reshape(2 * cols, rank)

        inverse = inverse_factor(jnp.reshape(place, (1,)).astype(jnp.int32), slabs)

        def solve(value):
            return jnp.einsum("rk,lk->rl", value, inverse, preferred_element_type=jnp.float32)

        reduced = solve(wide)
        squares = jnp.sum(reduced * reduced, axis=0, keepdims=True)
        squares = added(quad(squares, "col", col_count, experts))
        orthonormal = solve(projected).astype(jnp.bfloat16)

        def outer(right):
            value = jnp.einsum("rk,ck->rc", orthonormal, right, preferred_element_type=jnp.float32)
            return value[:, :cols], value[:, cols:]

        own, other = outer(reduced.astype(jnp.bfloat16))
        other = swap((0.1 * other).astype(jnp.bfloat16), "col", col_count, 1)
        momentum_new = buffer - pick(first, 0.1 * own, other.astype(jnp.float32))
        new_basis = (reduced * lax.rsqrt(squares + 1e-06)).astype(jnp.bfloat16)
        update_scale = math.sqrt(ROWS * COLS / RANK)
        own, other = outer(new_basis)
        own = (update_scale * own).astype(jnp.bfloat16)
        other = swap((update_scale * other).astype(jnp.bfloat16), "col", col_count, 1)
        return (momentum_new, pick(first, own, other))

    return local


def solution(mesh):
    placed = (P(None, "row", "col"), P(None, "row", "col"), P(None, "col", None))
    return jax.shard_map(
        make_local(mesh.shape["row"], mesh.shape["col"]),
        mesh=mesh,
        in_specs=placed,
        out_specs=(P(None, "row", "col"), P(None, "row", "col")),
        check_vma=False,
    )
```

```python
import functools
import math

import jax
import jax.numpy as jnp
import numpy as np
from jax import lax
from jax.experimental import pallas as pl
from jax.experimental.pallas import tpu as pltpu
from jax.sharding import Mesh
from jax.sharding import PartitionSpec as P

ROWS = 7168
COLS = 2048
RANK = 512
BLOCK = 128
PANEL = 8
BLOCKS = RANK // BLOCK
PANELS = BLOCK // PANEL
KEPT = 3
X_SIZE = 4
Z_SIZE = 8


def lanes_of(value, lane):
    return jnp.broadcast_to(value[:, lane : lane + 1], (PANEL, BLOCK))


def row_of(value, row):
    return jnp.broadcast_to(value[row : row + 1, :], (PANEL, BLOCK))


def added(terms):
    while len(terms) > 1:
        terms = [terms[i] + terms[i + 1] for i in range(0, len(terms), 2)]
    return terms[0]


def small_inverse(cols, row):
    cols = list(cols)
    factor = [jnp.zeros((PANEL, BLOCK), jnp.float32) for _ in range(PANEL)]
    for j in range(0, PANEL, 2):
        first, second = row == j, row == j + 1
        both = first | second
        left, right = cols[j], cols[j + 1]
        a, b, c = row_of(left, j), row_of(right, j), row_of(right, j + 1)
        root = lax.rsqrt(a * c - b * b)
        inv = root * root
        root_a = lax.rsqrt(a)
        ratio = b * (root_a * root_a)
        root_c = lax.rsqrt(c - b * ratio)
        left_m = jnp.where(first, -1.0, jnp.where(second, 0.0, left))
        right_m = jnp.where(first, 0.0, jnp.where(second, -1.0, right))
        for k in range(PANEL):
            if k in (j, j + 1):
                continue
            top, low = row_of(cols[k], j), row_of(cols[k], j + 1)
            rest = jnp.where(both, 0.0, cols[k])
            cols[k] = rest - inv * (left_m * (c * top - b * low) + right_m * (a * low - b * top))
            if k < j:
                factor[k] = jnp.where(
                    first, top * root_a, jnp.where(second, (low - ratio * top) * root_c, factor[k])
                )
        factor[j] = jnp.where(first, root_a, jnp.where(second, -(ratio * root_c), factor[j]))
        factor[j + 1] = jnp.where(second, root_c, factor[j + 1])
        cols[j] = inv * (right_m * b - left_m * c)
        cols[j + 1] = inv * (left_m * b - right_m * a)
    return cols, factor


def combine(cols, value):
    return added([cols[j] * row_of(value, j) for j in range(PANEL)])


def block_inverse_factor(groups, tasks):
    row = lax.broadcasted_iota(jnp.int32, (PANEL, BLOCK), 0)
    lane = lax.broadcasted_iota(jnp.int32, (PANEL, BLOCK), 1)
    block = [lanes_of(groups[0], j) for j in range(PANEL)]
    for k in range(PANELS):
        base = k * PANEL
        inside = (lane >= base) & (lane < base + PANEL)
        full, factor = small_inverse(block, row)
        panel = jnp.where(inside, (lane == row + base).astype(jnp.float32), groups[k])
        if k + 1 < PANELS:
            down = [lanes_of(groups[k + 1], base + j) for j in range(PANEL)]
            block = []
            for m in range(base + PANEL, base + 2 * PANEL):
                column = combine(full, lanes_of(groups[k], m))
                block.append(lanes_of(groups[k + 1], m) - combine(down, column))
            solved = combine(full, panel)
            rows = [row_of(solved, j) for j in range(PANEL)]
            for i in range(k + 1, PANELS):
                old = groups[i]
                change = added([lanes_of(old, base + j) * rows[j] for j in range(PANEL)])
                groups[i] = jnp.where(inside, 0.0, old) - change
        groups[k] = jnp.where(lane <= row + base, combine(factor, panel), 0.0)
        if k < len(tasks):
            tasks[k]()
    return groups


def split_halves(value):
    high = value.astype(jnp.bfloat16)
    low = (value - high.astype(jnp.float32)).astype(jnp.bfloat16)
    return high, low


def wide_terms(value):
    high, low = split_halves(value)
    return jnp.concatenate([high, high, low], axis=1)


def product(terms, right):
    high, low = split_halves(right)
    return jnp.dot(
        terms, jnp.concatenate([high, low, high], axis=0), preferred_element_type=jnp.float32
    )


def later_products(work_ref, k, inverse, columns):
    before, through = slice(0, k * BLOCK), slice(0, (k + 1) * BLOCK)
    lefts = {}

    def solve(j):
        upper = product(inverse, work_ref[k, :, columns(j)])
        work_ref[k, :, columns(j)] = upper
        lefts[j] = wide_terms(upper.T)

    def solve_before():
        work_ref[k, :, before] = product(inverse, work_ref[k, :, before])

    def update(i, j):
        work_ref[i, :, columns(j)] -= product(lefts[i], work_ref[k, :, columns(j)])

    def update_before(i):
        change = product(lefts[i], work_ref[k, :, through])
        if k > 0:
            work_ref[i, :, before] -= change[:, before]
        work_ref[i, :, columns(k)] = -change[:, columns(k)]

    rest = range(k + 1, BLOCKS)
    tasks = [functools.partial(solve, j) for j in rest[1:]]
    if k > 0:
        tasks.append(solve_before)
    for i in rest:
        tasks += [functools.partial(update, i, j) for j in range(i, BLOCKS) if j > k + 1]
        tasks.append(functools.partial(update_before, i))
    if k + 1 < BLOCKS:
        solve(k + 1)
        update(k + 1, k + 1)
        return tasks
    for task in tasks:
        task()
    return []


def factor_kernel(where_ref, own_ref, one_ref, two_ref, three_ref, out_ref, slab_ref, work_ref):
    here = where_ref[0]
    for back, ref in enumerate((own_ref, one_ref, two_ref, three_ref)):
        slab_ref[lax.rem(here + (BLOCKS - back), BLOCKS)] = ref[...]

    def block(i, j):
        if j - i < KEPT:
            return slab_ref[i, :, (j - i) * BLOCK : (j - i + 1) * BLOCK]
        return slab_ref[j, :, (BLOCKS + i - j) * BLOCK : (BLOCKS + i - j + 1) * BLOCK].T

    most = jnp.maximum(
        jnp.maximum(block(0, 0), block(1, 1)), jnp.maximum(block(2, 2), block(3, 3))
    )
    most = jnp.max(jnp.max(most, axis=0, keepdims=True), axis=1, keepdims=True)
    scale = 1.0 / most
    for i in range(BLOCKS):
        for j in range(i, BLOCKS):
            work_ref[i, :, j * BLOCK : (j + 1) * BLOCK] = block(i, j) * scale
    back_scale = lax.rsqrt(most)

    def columns(j):
        return slice(j * BLOCK, (j + 1) * BLOCK)

    tasks = []
    for k in range(BLOCKS):
        at, to = k * BLOCK, (k + 1) * BLOCK
        groups = [work_ref[k, i * PANEL : (i + 1) * PANEL, at:to] for i in range(PANELS)]
        inverse = jnp.concatenate(block_inverse_factor(groups, tasks), axis=0)
        work_ref[k, :, at:to] = inverse
        tasks = later_products(work_ref, k, wide_terms(inverse), columns)
    for i in range(BLOCKS):
        to = (i + 1) * BLOCK
        rows = slice(i * BLOCK, to)
        out_ref[rows, :to] = (work_ref[i, :, :to] * back_scale).astype(jnp.bfloat16)
        if to < RANK:
            out_ref[rows, to:] = jnp.zeros((BLOCK, RANK - to), jnp.bfloat16)


def inverse_factor(where, slabs):
    vmem = pl.BlockSpec(memory_space=pltpu.VMEM)
    return pl.pallas_call(
        factor_kernel,
        out_shape=jax.ShapeDtypeStruct((RANK, RANK), jnp.bfloat16),
        in_specs=[pl.BlockSpec(memory_space=pltpu.SMEM)] + [vmem] * BLOCKS,
        out_specs=vmem,
        scratch_shapes=[
            pltpu.VMEM((BLOCKS, BLOCK, KEPT * BLOCK), jnp.float32),
            pltpu.VMEM((BLOCKS, BLOCK, RANK), jnp.float32),
        ],
        compiler_params=pltpu.CompilerParams(vmem_limit_bytes=24 * 1024 * 1024),
        cost_estimate=pl.CostEstimate(flops=2 * 10**10, bytes_accessed=0, transcendentals=0),
    )(where, *slabs)


def place_kernel(where_ref, *refs):
    parts, out_ref = refs[:X_SIZE], refs[-1]
    for step, ref in enumerate(parts):
        out_ref[lax.bitwise_xor(where_ref[0], step)] = ref[...]


def placed_parts(where, parts):
    vmem = pl.BlockSpec(memory_space=pltpu.VMEM)
    return pl.pallas_call(
        place_kernel,
        out_shape=jax.ShapeDtypeStruct((X_SIZE,) + parts[0].shape, parts[0].dtype),
        in_specs=[pl.BlockSpec(memory_space=pltpu.SMEM)] + [vmem] * X_SIZE,
        out_specs=vmem,
    )(where, *parts)


def wide_kernel(own_ref, other_ref, right_ref, _, out_ref):
    for i, ref in enumerate((own_ref, other_ref)):
        out_ref[i] = lax.dot_general(
            ref[...], right_ref[...], (((0,), (0,)), ((), ())), preferred_element_type=jnp.float32
        ).astype(out_ref.dtype)


def wide_product(own, other, right, after):
    vmem = pl.BlockSpec(memory_space=pltpu.VMEM)
    return pl.pallas_call(
        wide_kernel,
        out_shape=jax.ShapeDtypeStruct((2, own.shape[1], right.shape[1]), jnp.bfloat16),
        in_specs=[vmem] * 4,
        out_specs=vmem,
        compiler_params=pltpu.CompilerParams(vmem_limit_bytes=24 * 1024 * 1024),
    )(own, other, right, after)


def solve_kernel(where_ref, inverse_ref, wide_ref, out_ref, squares_ref):
    squares = jnp.zeros(squares_ref.shape, jnp.float32)
    for step in range(X_SIZE):
        rows = wide_ref[:, step].reshape(out_ref.shape[1:])
        value = lax.dot_general(
            rows, inverse_ref[...], (((1,), (1,)), ((), ())), preferred_element_type=jnp.float32
        )
        out_ref[lax.bitwise_xor(where_ref[0], step)] = value
        squares += jnp.sum(value * value, axis=0, keepdims=True)
    squares_ref[...] = squares


def solved_rows(where, inverse, wide):
    vmem = pl.BlockSpec(memory_space=pltpu.VMEM)
    return pl.pallas_call(
        solve_kernel,
        out_shape=(
            jax.ShapeDtypeStruct((X_SIZE, Z_SIZE * wide.shape[2], RANK), jnp.float32),
            jax.ShapeDtypeStruct((1, RANK), jnp.float32),
        ),
        in_specs=[pl.BlockSpec(memory_space=pltpu.SMEM), vmem, vmem],
        out_specs=(vmem, vmem),
        compiler_params=pltpu.CompilerParams(vmem_limit_bytes=24 * 1024 * 1024),
    )(where, inverse, wide)


def sum_kernel(*refs):
    terms = [ref[...].astype(jnp.float32) for ref in refs[:-2]]
    refs[-1][...] = added(terms).astype(refs[-1].dtype)


def summed(terms, after):
    vmem = pl.BlockSpec(memory_space=pltpu.VMEM)
    return pl.pallas_call(
        sum_kernel,
        out_shape=jax.ShapeDtypeStruct(terms[0].shape, terms[0].dtype),
        in_specs=[vmem] * (len(terms) + 1),
        out_specs=vmem,
    )(*terms, after)


SIZES = {"x": X_SIZE, "z": Z_SIZE, "y": BLOCKS, "core": 2}


def spread(chunks, axis):
    return lax.all_to_all(chunks, axis, split_axis=0, concat_axis=0, tiled=True)


def swap(value, axis, mask=1):
    return lax.ppermute(value, axis, [(i, i ^ mask) for i in range(SIZES[axis])])


def quad(value, axis):
    return [value] + [swap(value, axis, step) for step in (1, 2, 3)]


def pick(first, value, other):
    return jnp.stack([jnp.where(first, value, other), jnp.where(first, other, value)])


def item(stack, index):
    return lax.dynamic_index_in_dim(stack, index, 0, keepdims=False)


def x_terms(value, plane):
    pieces = value.reshape(X_SIZE, value.shape[0] // X_SIZE, value.shape[1])
    terms = [item(pieces, plane)]
    for step in range(1, X_SIZE):
        send = item(pieces, lax.bitwise_xor(plane, np.uint32(step)))
        terms.append(swap(send, "x", step))
    return terms


def local(momentum, gradient, basis_in):
    experts, rows, cols = momentum.shape
    rank = basis_in.shape[-1]
    expert = lax.axis_index("core").astype(jnp.uint32)
    place = lax.axis_index("y").astype(jnp.uint32)
    plane = lax.axis_index("x").astype(jnp.uint32)
    where_y = jnp.reshape(place, (1,)).astype(jnp.int32)
    where_x = jnp.reshape(plane, (1,)).astype(jnp.int32)
    first = expert == 0
    buffer = lax.optimization_barrier(momentum + gradient.astype(jnp.float32))
    half = buffer.astype(jnp.bfloat16)
    partial = jnp.einsum(
        "erc,eck->erk", half, basis_in, preferred_element_type=jnp.float32
    ).astype(jnp.bfloat16)
    term = item(partial, expert) + swap(item(partial, 1 - expert), "core")
    projected = added([part.astype(jnp.float32) for part in quad(term, "y")]).astype(jnp.bfloat16)

    turned = lax.dynamic_slice_in_dim(
        jnp.concatenate([projected, projected[:, : (KEPT - 1) * BLOCK]], axis=1),
        place * np.uint32(BLOCK),
        KEPT * BLOCK,
        axis=1,
    )
    gram = jnp.einsum("rk,rl->kl", turned[:, :BLOCK], turned, preferred_element_type=jnp.float32)
    gram = added(x_terms(gram, plane))

    left = swap(item(half, 1 - expert), "core")
    wide = wide_product(item(half, expert), left, projected, gram[:PANEL, :BLOCK])
    terms = x_terms(wide.reshape(2 * cols, rank), plane)

    gram = gram + swap(gram, "z", 4)
    gram = added(quad(gram, "z"))
    wide = summed(terms, gram[:PANEL, :BLOCK])
    wide = spread(wide.reshape(Z_SIZE, 2 * cols // (X_SIZE * Z_SIZE), rank), "z")
    wide = jnp.sum(wide.astype(jnp.float32), axis=0).astype(jnp.bfloat16)
    wide = jnp.stack(quad(wide, "x"))
    wide = spread(jnp.broadcast_to(wide[None], (Z_SIZE,) + wide.shape), "z")

    slab = placed_parts(where_x, quad(gram, "x")).reshape(BLOCK, KEPT * BLOCK)
    slabs = [slab]
    for step in range(1, BLOCKS):
        slabs.append(lax.ppermute(slab, "y", [(i, (i + step) % BLOCKS) for i in range(BLOCKS)]))

    inverse = inverse_factor(where_y, slabs)
    reduced, squares = solved_rows(where_x, inverse, wide)
    reduced = reduced.reshape(2 * cols, rank)
    squares = added(quad(squares, "y"))
    orthonormal = jnp.einsum(
        "rk,lk->rl", projected, inverse, preferred_element_type=jnp.float32
    ).astype(jnp.bfloat16)

    def outer(right):
        value = jnp.einsum("rk,ck->rc", orthonormal, right, preferred_element_type=jnp.float32)
        return value[:, :cols], value[:, cols:]

    own, other = outer(reduced.astype(jnp.bfloat16))
    other = swap((0.1 * other).astype(jnp.bfloat16), "core")
    momentum_new = buffer - pick(first, 0.1 * own, other.astype(jnp.float32))
    new_basis = (reduced * lax.rsqrt(squares + 1e-06)).astype(jnp.bfloat16)
    update_scale = math.sqrt(ROWS * COLS / RANK)
    own, other = outer(new_basis)
    own = (update_scale * own).astype(jnp.bfloat16)
    other = swap((update_scale * other).astype(jnp.bfloat16), "core")
    return (momentum_new, pick(first, own, other))


def solution(mesh):
    lines = Mesh(mesh.devices.reshape(X_SIZE, Z_SIZE, BLOCKS, 2), ("x", "z", "y", "core"))
    placed = P(None, ("x", "z"), ("y", "core"))
    return jax.shard_map(
        local,
        mesh=lines,
        in_specs=(placed, placed, P(None, ("y", "core"), None)),
        out_specs=(placed, placed),
        check_vma=False,
    )
```

```python
import functools
import math

import jax
import jax.numpy as jnp
import numpy as np
from jax import lax
from jax.experimental import pallas as pl
from jax.experimental.pallas import tpu as pltpu
from jax.sharding import Mesh
from jax.sharding import PartitionSpec as P

ROWS = 7168
COLS = 2048
RANK = 512
BLOCK = 128
PANEL = 8
BLOCKS = RANK // BLOCK
PANELS = BLOCK // PANEL
KEPT = 3
X_SIZE = 4
Z_SIZE = 8


def lanes_of(value, lane):
    return jnp.broadcast_to(value[:, lane : lane + 1], (PANEL, BLOCK))


def row_of(value, row):
    return jnp.broadcast_to(value[row : row + 1, :], (PANEL, BLOCK))


def added(terms):
    while len(terms) > 1:
        terms = [terms[i] + terms[i + 1] for i in range(0, len(terms), 2)]
    return terms[0]


def small_inverse(cols, row):
    cols = list(cols)
    factor = [jnp.zeros((PANEL, BLOCK), jnp.float32) for _ in range(PANEL)]
    for j in range(0, PANEL, 2):
        first, second = row == j, row == j + 1
        both = first | second
        left, right = cols[j], cols[j + 1]
        a, b, c = row_of(left, j), row_of(right, j), row_of(right, j + 1)
        root = lax.rsqrt(a * c - b * b)
        inv = root * root
        root_a = lax.rsqrt(a)
        ratio = b * (root_a * root_a)
        root_c = lax.rsqrt(c - b * ratio)
        left_m = jnp.where(first, -1.0, jnp.where(second, 0.0, left))
        right_m = jnp.where(first, 0.0, jnp.where(second, -1.0, right))
        for k in range(PANEL):
            if k in (j, j + 1):
                continue
            top, low = row_of(cols[k], j), row_of(cols[k], j + 1)
            rest = jnp.where(both, 0.0, cols[k])
            cols[k] = rest - inv * (left_m * (c * top - b * low) + right_m * (a * low - b * top))
            if k < j:
                factor[k] = jnp.where(
                    first, top * root_a, jnp.where(second, (low - ratio * top) * root_c, factor[k])
                )
        factor[j] = jnp.where(first, root_a, jnp.where(second, -(ratio * root_c), factor[j]))
        factor[j + 1] = jnp.where(second, root_c, factor[j + 1])
        cols[j] = inv * (right_m * b - left_m * c)
        cols[j + 1] = inv * (left_m * b - right_m * a)
    return cols, factor


def combine(cols, value):
    return added([cols[j] * row_of(value, j) for j in range(PANEL)])


def block_inverse_factor(groups, tasks):
    row = lax.broadcasted_iota(jnp.int32, (PANEL, BLOCK), 0)
    lane = lax.broadcasted_iota(jnp.int32, (PANEL, BLOCK), 1)
    block = [lanes_of(groups[0], j) for j in range(PANEL)]
    for k in range(PANELS):
        base = k * PANEL
        inside = (lane >= base) & (lane < base + PANEL)
        full, factor = small_inverse(block, row)
        panel = jnp.where(inside, (lane == row + base).astype(jnp.float32), groups[k])
        if k + 1 < PANELS:
            down = [lanes_of(groups[k + 1], base + j) for j in range(PANEL)]
            block = []
            for m in range(base + PANEL, base + 2 * PANEL):
                column = combine(full, lanes_of(groups[k], m))
                block.append(lanes_of(groups[k + 1], m) - combine(down, column))
            solved = combine(full, panel)
            rows = [row_of(solved, j) for j in range(PANEL)]
            for i in range(k + 1, PANELS):
                old = groups[i]
                change = added([lanes_of(old, base + j) * rows[j] for j in range(PANEL)])
                groups[i] = jnp.where(inside, 0.0, old) - change
        groups[k] = jnp.where(lane <= row + base, combine(factor, panel), 0.0)
        if k < len(tasks):
            tasks[k]()
    return groups


def split_halves(value):
    high = value.astype(jnp.bfloat16)
    low = (value - high.astype(jnp.float32)).astype(jnp.bfloat16)
    return high, low


def wide_terms(value):
    high, low = split_halves(value)
    return jnp.concatenate([high, high, low], axis=1)


def product(terms, right):
    high, low = split_halves(right)
    return jnp.dot(
        terms, jnp.concatenate([high, low, high], axis=0), preferred_element_type=jnp.float32
    )


def later_products(work_ref, k, inverse, columns):
    before, through = slice(0, k * BLOCK), slice(0, (k + 1) * BLOCK)
    lefts = {}

    def solve(j):
        upper = product(inverse, work_ref[k, :, columns(j)])
        work_ref[k, :, columns(j)] = upper
        lefts[j] = wide_terms(upper.T)

    def solve_before():
        work_ref[k, :, before] = product(inverse, work_ref[k, :, before])

    def update(i, j):
        work_ref[i, :, columns(j)] -= product(lefts[i], work_ref[k, :, columns(j)])

    def update_before(i):
        change = product(lefts[i], work_ref[k, :, through])
        if k > 0:
            work_ref[i, :, before] -= change[:, before]
        work_ref[i, :, columns(k)] = -change[:, columns(k)]

    rest = range(k + 1, BLOCKS)
    tasks = [functools.partial(solve, j) for j in rest[1:]]
    if k > 0:
        tasks.append(solve_before)
    for i in rest:
        tasks += [functools.partial(update, i, j) for j in range(i, BLOCKS) if j > k + 1]
        tasks.append(functools.partial(update_before, i))
    if k + 1 < BLOCKS:
        solve(k + 1)
        update(k + 1, k + 1)
        return tasks
    for task in tasks:
        task()
    return []


def factor_kernel(where_ref, own_ref, one_ref, two_ref, three_ref, out_ref, slab_ref, work_ref):
    here = where_ref[0]
    for back, ref in enumerate((own_ref, one_ref, two_ref, three_ref)):
        slab_ref[lax.rem(here + (BLOCKS - back), BLOCKS)] = ref[...]

    def block(i, j):
        if j - i < KEPT:
            return slab_ref[i, :, (j - i) * BLOCK : (j - i + 1) * BLOCK]
        return slab_ref[j, :, (BLOCKS + i - j) * BLOCK : (BLOCKS + i - j + 1) * BLOCK].T

    most = jnp.maximum(
        jnp.maximum(block(0, 0), block(1, 1)), jnp.maximum(block(2, 2), block(3, 3))
    )
    most = jnp.max(jnp.max(most, axis=0, keepdims=True), axis=1, keepdims=True)
    scale = 1.0 / most
    for i in range(BLOCKS):
        for j in range(i, BLOCKS):
            work_ref[i, :, j * BLOCK : (j + 1) * BLOCK] = block(i, j) * scale
    back_scale = lax.rsqrt(most)

    def columns(j):
        return slice(j * BLOCK, (j + 1) * BLOCK)

    tasks = []
    for k in range(BLOCKS):
        at, to = k * BLOCK, (k + 1) * BLOCK
        groups = [work_ref[k, i * PANEL : (i + 1) * PANEL, at:to] for i in range(PANELS)]
        inverse = jnp.concatenate(block_inverse_factor(groups, tasks), axis=0)
        work_ref[k, :, at:to] = inverse
        tasks = later_products(work_ref, k, wide_terms(inverse), columns)
    for i in range(BLOCKS):
        to = (i + 1) * BLOCK
        rows = slice(i * BLOCK, to)
        out_ref[rows, :to] = (work_ref[i, :, :to] * back_scale).astype(jnp.bfloat16)
        if to < RANK:
            out_ref[rows, to:] = jnp.zeros((BLOCK, RANK - to), jnp.bfloat16)


def inverse_factor(where, slabs):
    vmem = pl.BlockSpec(memory_space=pltpu.VMEM)
    return pl.pallas_call(
        factor_kernel,
        out_shape=jax.ShapeDtypeStruct((RANK, RANK), jnp.bfloat16),
        in_specs=[pl.BlockSpec(memory_space=pltpu.SMEM)] + [vmem] * BLOCKS,
        out_specs=vmem,
        scratch_shapes=[
            pltpu.VMEM((BLOCKS, BLOCK, KEPT * BLOCK), jnp.float32),
            pltpu.VMEM((BLOCKS, BLOCK, RANK), jnp.float32),
        ],
        compiler_params=pltpu.CompilerParams(vmem_limit_bytes=24 * 1024 * 1024),
        cost_estimate=pl.CostEstimate(flops=2 * 10**10, bytes_accessed=0, transcendentals=0),
    )(where, *slabs)


SIZES = {"x": X_SIZE, "z": Z_SIZE, "y": BLOCKS, "core": 2}


def spread(chunks, axis):
    return lax.all_to_all(chunks, axis, split_axis=0, concat_axis=0, tiled=True)


def swap(value, axis, mask=1):
    return lax.ppermute(value, axis, [(i, i ^ mask) for i in range(SIZES[axis])])


def quad(value, axis):
    return [value] + [swap(value, axis, step) for step in (1, 2, 3)]


def pick(first, value, other):
    return jnp.stack([jnp.where(first, value, other), jnp.where(first, other, value)])


def item(stack, index):
    return lax.dynamic_index_in_dim(stack, index, 0, keepdims=False)


def x_terms(value, plane):
    pieces = value.reshape(X_SIZE, value.shape[0] // X_SIZE, value.shape[1])
    terms = [item(pieces, plane)]
    for step in range(1, X_SIZE):
        send = item(pieces, lax.bitwise_xor(plane, np.uint32(step)))
        terms.append(swap(send, "x", step))
    return terms


def local(momentum, gradient, basis_in):
    experts, rows, cols = momentum.shape
    rank = basis_in.shape[-1]
    expert = lax.axis_index("core").astype(jnp.uint32)
    place = lax.axis_index("y").astype(jnp.uint32)
    plane = lax.axis_index("x").astype(jnp.uint32)
    first = expert == 0
    buffer = lax.optimization_barrier(momentum + gradient.astype(jnp.float32))
    half = buffer.astype(jnp.bfloat16)
    partial = jnp.einsum(
        "erc,eck->erk", half, basis_in, preferred_element_type=jnp.float32
    ).astype(jnp.bfloat16)
    term = item(partial, expert) + swap(item(partial, 1 - expert), "core")
    upper, lower = term[: rows // 2], term[rows // 2 :]
    upper, lower = upper + swap(upper, "y", 1), lower + swap(lower, "y", 3)
    upper, lower = upper + swap(upper, "y", 3), lower + swap(lower, "y", 1)
    projected = jnp.concatenate([upper, lower], axis=0)

    turned = lax.dynamic_slice_in_dim(
        jnp.concatenate([projected, projected[:, : (KEPT - 1) * BLOCK]], axis=1),
        place * np.uint32(BLOCK),
        KEPT * BLOCK,
        axis=1,
    )
    gram = jnp.einsum("rk,rl->kl", turned[:, :BLOCK], turned, preferred_element_type=jnp.float32)
    gram = added(x_terms(gram, plane))

    gram = gram + swap(gram, "z", 4)
    gram = added(quad(gram, "z"))
    parts = quad(gram, "x")
    low = lax.bitwise_and(plane, np.uint32(1)) == 0
    slab = pick(
        plane < np.uint32(2), pick(low, parts[0], parts[1]), pick(low, parts[2], parts[3])
    ).reshape(BLOCK, KEPT * BLOCK)
    slabs = [slab]
    for step in range(1, BLOCKS):
        slabs.append(lax.ppermute(slab, "y", [(i, (i + step) % BLOCKS) for i in range(BLOCKS)]))

    whole = jnp.stack([item(half, expert), swap(item(half, 1 - expert), "core")])
    wide = jnp.einsum("hrc,rk->hck", whole, projected, preferred_element_type=jnp.float32)
    row_count = X_SIZE * Z_SIZE
    wide = wide.astype(jnp.bfloat16).reshape(row_count, 2 * cols // row_count, rank)
    wide = jnp.sum(spread(wide, ("x", "z")).astype(jnp.float32), axis=0).astype(jnp.bfloat16)
    wide = spread(jnp.broadcast_to(wide[None], (row_count,) + wide.shape), ("x", "z"))

    inverse = inverse_factor(jnp.reshape(place, (1,)).astype(jnp.int32), slabs)

    def solve(value):
        return jnp.einsum("rk,lk->rl", value, inverse, preferred_element_type=jnp.float32)

    reduced = solve(wide.reshape(2 * cols, rank))
    squares = added(quad(jnp.sum(reduced * reduced, axis=0, keepdims=True), "y"))
    orthonormal = solve(projected).astype(jnp.bfloat16)

    def outer(right):
        value = jnp.einsum("rk,ck->rc", orthonormal, right, preferred_element_type=jnp.float32)
        return value[:, :cols], value[:, cols:]

    own, other = outer(reduced.astype(jnp.bfloat16))
    other = swap((0.1 * other).astype(jnp.bfloat16), "core")
    momentum_new = buffer - pick(first, 0.1 * own, other.astype(jnp.float32))
    new_basis = (reduced * lax.rsqrt(squares + 1e-06)).astype(jnp.bfloat16)
    update_scale = math.sqrt(ROWS * COLS / RANK)
    own, other = outer(new_basis)
    own = (update_scale * own).astype(jnp.bfloat16)
    other = swap((update_scale * other).astype(jnp.bfloat16), "core")
    return (momentum_new, pick(first, own, other))


def solution(mesh):
    lines = Mesh(mesh.devices.reshape(X_SIZE, Z_SIZE, BLOCKS, 2), ("x", "z", "y", "core"))
    placed = P(None, ("x", "z"), ("y", "core"))
    return jax.shard_map(
        local,
        mesh=lines,
        in_specs=(placed, placed, P(None, ("y", "core"), None)),
        out_specs=(placed, placed),
        check_vma=False,
    )
```

```python
import functools
import math

import jax
import jax.numpy as jnp
import numpy as np
from jax import lax
from jax.experimental import pallas as pl
from jax.experimental.pallas import tpu as pltpu
from jax.sharding import Mesh
from jax.sharding import PartitionSpec as P

ROWS = 7168
COLS = 2048
RANK = 512
BLOCK = 128
PANEL = 8
BLOCKS = RANK // BLOCK
PANELS = BLOCK // PANEL
KEPT = 3
AHEAD = 4
X_SIZE = 4
Z_SIZE = 8


def lanes_of(value, lane):
    return jnp.broadcast_to(value[:, lane : lane + 1], (PANEL, BLOCK))


def row_of(value, row):
    return jnp.broadcast_to(value[row : row + 1, :], (PANEL, BLOCK))


def added(terms):
    while len(terms) > 1:
        terms = [terms[i] + terms[i + 1] for i in range(0, len(terms), 2)]
    return terms[0]


def small_inverse(cols, row):
    cols = list(cols)
    factor = [jnp.zeros((PANEL, BLOCK), jnp.float32) for _ in range(PANEL)]
    for j in range(0, PANEL, 2):
        first, second = row == j, row == j + 1
        both = first | second
        left, right = cols[j], cols[j + 1]
        a, b, c = row_of(left, j), row_of(right, j), row_of(right, j + 1)
        root = lax.rsqrt(a * c - b * b)
        inv = root * root
        root_a = lax.rsqrt(a)
        ratio = b * (root_a * root_a)
        root_c = lax.rsqrt(c - b * ratio)
        left = jnp.where(first, -1.0, jnp.where(second, 0.0, left))
        right = jnp.where(first, 0.0, jnp.where(second, -1.0, right))
        alpha, beta = left * c - right * b, right * a - left * b
        for k in range(PANEL):
            if k in (j, j + 1):
                continue
            top, low = row_of(cols[k], j), row_of(cols[k], j + 1)
            cols[k] = jnp.where(both, 0.0, cols[k]) - inv * (alpha * top + beta * low)
            if k < j:
                factor[k] = jnp.where(
                    first, top * root_a, jnp.where(second, (low - ratio * top) * root_c, factor[k])
                )
        factor[j] = jnp.where(first, root_a, jnp.where(second, -(ratio * root_c), factor[j]))
        factor[j + 1] = jnp.where(second, root_c, factor[j + 1])
        cols[j] = -(inv * alpha)
        cols[j + 1] = -(inv * beta)
    return cols, factor


def combine(cols, value):
    return added([cols[j] * row_of(value, j) for j in range(PANEL)])


def block_inverse_factor(groups, tasks):
    row = lax.broadcasted_iota(jnp.int32, (PANEL, BLOCK), 0)
    lane = lax.broadcasted_iota(jnp.int32, (PANEL, BLOCK), 1)
    block = [lanes_of(groups[0], j) for j in range(PANEL)]
    for k in range(PANELS):
        base = k * PANEL
        inside = (lane >= base) & (lane < base + PANEL)
        full, factor = small_inverse(block, row)
        panel = jnp.where(inside, (lane == row + base).astype(jnp.float32), groups[k])
        if k + 1 < PANELS:
            down = [lanes_of(groups[k + 1], base + j) for j in range(PANEL)]
            block = []
            for m in range(base + PANEL, base + PANEL + AHEAD):
                column = combine(full, lanes_of(groups[k], m))
                block.append(lanes_of(groups[k + 1], m) - combine(down, column))
            solved = combine(full, panel)
            rows = [row_of(solved, j) for j in range(PANEL)]
            for i in range(k + 1, PANELS):
                old = groups[i]
                change = added([lanes_of(old, base + j) * rows[j] for j in range(PANEL)])
                groups[i] = jnp.where(inside, 0.0, old) - change
            for m in range(base + PANEL + AHEAD, base + 2 * PANEL):
                block.append(lanes_of(groups[k + 1], m))
        groups[k] = jnp.where(lane <= row + base, combine(factor, panel), 0.0)
        if k < len(tasks):
            tasks[k]()
    return groups


def split_halves(value):
    high = value.astype(jnp.bfloat16)
    low = (value - high.astype(jnp.float32)).astype(jnp.bfloat16)
    return high, low


def wide_terms(value):
    high, low = split_halves(value)
    return jnp.concatenate([high, high, low], axis=1)


def product(terms, right):
    high, low = split_halves(right)
    return jnp.dot(
        terms, jnp.concatenate([high, low, high], axis=0), preferred_element_type=jnp.float32
    )


def later_products(work_ref, k, inverse, columns):
    before, through = slice(0, k * BLOCK), slice(0, (k + 1) * BLOCK)
    lefts = {}

    def solve(j):
        upper = product(inverse, work_ref[k, :, columns(j)])
        work_ref[k, :, columns(j)] = upper
        lefts[j] = wide_terms(upper.T)

    def solve_before():
        work_ref[k, :, before] = product(inverse, work_ref[k, :, before])

    def update(i, j):
        work_ref[i, :, columns(j)] -= product(lefts[i], work_ref[k, :, columns(j)])

    def update_before(i):
        change = product(lefts[i], work_ref[k, :, through])
        if k > 0:
            work_ref[i, :, before] -= change[:, before]
        work_ref[i, :, columns(k)] = -change[:, columns(k)]

    rest = range(k + 1, BLOCKS)
    tasks = [functools.partial(solve, j) for j in rest[1:]]
    if k > 0:
        tasks.append(solve_before)
    for i in rest:
        tasks += [functools.partial(update, i, j) for j in range(i, BLOCKS) if j > k + 1]
        tasks.append(functools.partial(update_before, i))
    if k + 1 < BLOCKS:
        solve(k + 1)
        update(k + 1, k + 1)
        return tasks
    for task in tasks:
        task()
    return []


def factor_kernel(where_ref, own_ref, one_ref, two_ref, three_ref, out_ref, slab_ref, work_ref):
    here = where_ref[0]
    for back, ref in enumerate((own_ref, one_ref, two_ref, three_ref)):
        slab_ref[lax.rem(here + (BLOCKS - back), BLOCKS)] = ref[...]

    def block(i, j):
        if j - i < KEPT:
            return slab_ref[i, :, (j - i) * BLOCK : (j - i + 1) * BLOCK]
        return slab_ref[j, :, (BLOCKS + i - j) * BLOCK : (BLOCKS + i - j + 1) * BLOCK].T

    most = jnp.maximum(
        jnp.maximum(block(0, 0), block(1, 1)), jnp.maximum(block(2, 2), block(3, 3))
    )
    most = jnp.max(jnp.max(most, axis=0, keepdims=True), axis=1, keepdims=True)
    scale = 1.0 / most
    for i in range(BLOCKS):
        for j in range(i, BLOCKS):
            work_ref[i, :, j * BLOCK : (j + 1) * BLOCK] = block(i, j) * scale
    back_scale = lax.rsqrt(most)

    def columns(j):
        return slice(j * BLOCK, (j + 1) * BLOCK)

    tasks = []
    for k in range(BLOCKS):
        at, to = k * BLOCK, (k + 1) * BLOCK
        groups = [work_ref[k, i * PANEL : (i + 1) * PANEL, at:to] for i in range(PANELS)]
        inverse = jnp.concatenate(block_inverse_factor(groups, tasks), axis=0)
        work_ref[k, :, at:to] = inverse
        tasks = later_products(work_ref, k, wide_terms(inverse), columns)
    for i in range(BLOCKS):
        to = (i + 1) * BLOCK
        rows = slice(i * BLOCK, to)
        out_ref[rows, :to] = (work_ref[i, :, :to] * back_scale).astype(jnp.bfloat16)
        if to < RANK:
            out_ref[rows, to:] = jnp.zeros((BLOCK, RANK - to), jnp.bfloat16)


def inverse_factor(where, slabs):
    vmem = pl.BlockSpec(memory_space=pltpu.VMEM)
    return pl.pallas_call(
        factor_kernel,
        out_shape=jax.ShapeDtypeStruct((RANK, RANK), jnp.bfloat16),
        in_specs=[pl.BlockSpec(memory_space=pltpu.SMEM)] + [vmem] * BLOCKS,
        out_specs=vmem,
        scratch_shapes=[
            pltpu.VMEM((BLOCKS, BLOCK, KEPT * BLOCK), jnp.float32),
            pltpu.VMEM((BLOCKS, BLOCK, RANK), jnp.float32),
        ],
        compiler_params=pltpu.CompilerParams(vmem_limit_bytes=24 * 1024 * 1024),
        cost_estimate=pl.CostEstimate(flops=2 * 10**10, bytes_accessed=0, transcendentals=0),
    )(where, *slabs)


SIZES = {"x": X_SIZE, "z": Z_SIZE, "y": BLOCKS, "core": 2}


def spread(chunks, axis):
    return lax.all_to_all(chunks, axis, split_axis=0, concat_axis=0, tiled=True)


def swap(value, axis, mask=1):
    return lax.ppermute(value, axis, [(i, i ^ mask) for i in range(SIZES[axis])])


def quad(value, axis):
    return [value] + [swap(value, axis, step) for step in (1, 2, 3)]


def pick(first, value, other):
    return jnp.stack([jnp.where(first, value, other), jnp.where(first, other, value)])


def item(stack, index):
    return lax.dynamic_index_in_dim(stack, index, 0, keepdims=False)


def x_terms(value, plane):
    pieces = value.reshape(X_SIZE, value.shape[0] // X_SIZE, value.shape[1])
    terms = [item(pieces, plane)]
    for step in range(1, X_SIZE):
        send = item(pieces, lax.bitwise_xor(plane, np.uint32(step)))
        terms.append(swap(send, "x", step))
    return terms


def local(momentum, gradient, basis_in):
    experts, rows, cols = momentum.shape
    rank = basis_in.shape[-1]
    expert = lax.axis_index("core").astype(jnp.uint32)
    place = lax.axis_index("y").astype(jnp.uint32)
    plane = lax.axis_index("x").astype(jnp.uint32)
    first = expert == 0
    buffer = lax.optimization_barrier(momentum + gradient.astype(jnp.float32))
    half = buffer.astype(jnp.bfloat16)
    partial = jnp.einsum(
        "erc,eck->erk", half, basis_in, preferred_element_type=jnp.float32
    ).astype(jnp.bfloat16)
    term = item(partial, expert) + swap(item(partial, 1 - expert), "core")
    upper, lower = term[: rows // 2], term[rows // 2 :]
    upper, lower = upper + swap(upper, "y", 1), lower + swap(lower, "y", 3)
    upper, lower = upper + swap(upper, "y", 3), lower + swap(lower, "y", 1)
    projected = jnp.concatenate([upper, lower], axis=0)

    turned = lax.dynamic_slice_in_dim(
        jnp.concatenate([projected, projected[:, : (KEPT - 1) * BLOCK]], axis=1),
        place * np.uint32(BLOCK),
        KEPT * BLOCK,
        axis=1,
    )
    gram = jnp.einsum("rk,rl->kl", turned[:, :BLOCK], turned, preferred_element_type=jnp.float32)
    gram = added(x_terms(gram, plane))

    gram = gram + swap(gram, "z", 4)
    gram = added(quad(gram, "z"))
    parts = quad(gram, "x")
    low = lax.bitwise_and(plane, np.uint32(1)) == 0
    slab = pick(
        plane < np.uint32(2), pick(low, parts[0], parts[1]), pick(low, parts[2], parts[3])
    ).reshape(BLOCK, KEPT * BLOCK)
    slabs = [slab]
    for step in range(1, BLOCKS):
        slabs.append(lax.ppermute(slab, "y", [(i, (i + step) % BLOCKS) for i in range(BLOCKS)]))

    whole = jnp.stack([item(half, expert), swap(item(half, 1 - expert), "core")])
    wide = jnp.einsum("hrc,rk->hck", whole, projected, preferred_element_type=jnp.float32)
    row_count = X_SIZE * Z_SIZE
    wide = wide.astype(jnp.bfloat16).reshape(row_count, 2 * cols // row_count, rank)
    wide = jnp.sum(spread(wide, ("x", "z")).astype(jnp.float32), axis=0).astype(jnp.bfloat16)
    wide = spread(jnp.broadcast_to(wide[None], (row_count,) + wide.shape), ("x", "z"))

    inverse = inverse_factor(jnp.reshape(place, (1,)).astype(jnp.int32), slabs)

    def solve(value):
        return jnp.einsum("rk,lk->rl", value, inverse, preferred_element_type=jnp.float32)

    reduced = solve(wide.reshape(2 * cols, rank))
    squares = added(quad(jnp.sum(reduced * reduced, axis=0, keepdims=True), "y"))
    orthonormal = solve(projected).astype(jnp.bfloat16)

    def outer(right):
        value = jnp.einsum("rk,ck->rc", orthonormal, right, preferred_element_type=jnp.float32)
        return value[:, :cols], value[:, cols:]

    own, other = outer(reduced.astype(jnp.bfloat16))
    other = swap((0.1 * other).astype(jnp.bfloat16), "core")
    momentum_new = buffer - pick(first, 0.1 * own, other.astype(jnp.float32))
    new_basis = (reduced * lax.rsqrt(squares + 1e-06)).astype(jnp.bfloat16)
    update_scale = math.sqrt(ROWS * COLS / RANK)
    own, other = outer(new_basis)
    own = (update_scale * own).astype(jnp.bfloat16)
    other = swap((update_scale * other).astype(jnp.bfloat16), "core")
    return (momentum_new, pick(first, own, other))


def solution(mesh):
    lines = Mesh(mesh.devices.reshape(X_SIZE, Z_SIZE, BLOCKS, 2), ("x", "z", "y", "core"))
    placed = P(None, ("x", "z"), ("y", "core"))
    return jax.shard_map(
        local,
        mesh=lines,
        in_specs=(placed, placed, P(None, ("y", "core"), None)),
        out_specs=(placed, placed),
        check_vma=False,
    )
```

```python
import functools
import math

import jax
import jax.numpy as jnp
import numpy as np
from jax import lax
from jax.experimental import pallas as pl
from jax.experimental.pallas import tpu as pltpu
from jax.sharding import Mesh
from jax.sharding import PartitionSpec as P

ROWS = 7168
COLS = 2048
RANK = 512
BLOCK = 128
PANEL = 8
BLOCKS = RANK // BLOCK
PANELS = BLOCK // PANEL
KEPT = 3
AHEAD = 8
X_SIZE = 4
Z_SIZE = 8


def lanes_of(value, lane):
    return jnp.broadcast_to(value[:, lane : lane + 1], (PANEL, BLOCK))


def row_of(value, row):
    return jnp.broadcast_to(value[row : row + 1, :], (PANEL, BLOCK))


def added(terms):
    while len(terms) > 1:
        terms = [terms[i] + terms[i + 1] for i in range(0, len(terms), 2)]
    return terms[0]


def small_inverse(cols, row):
    cols = list(cols)
    factor = [jnp.zeros((PANEL, BLOCK), jnp.float32) for _ in range(PANEL)]
    for j in range(0, PANEL, 2):
        first, second = row == j, row == j + 1
        both = first | second
        left, right = cols[j], cols[j + 1]
        if j == 0:
            a, b, c = row_of(left, 0), row_of(right, 0), row_of(right, 1)
        root = lax.rsqrt(a * c - b * b)
        inv = root * root
        root_a = lax.rsqrt(a)
        ratio = b * (root_a * root_a)
        root_c = lax.rsqrt(c - b * ratio)
        left = jnp.where(first, -1.0, jnp.where(second, 0.0, left))
        right = jnp.where(first, 0.0, jnp.where(second, -1.0, right))
        alpha, beta = left * c - right * b, right * a - left * b

        def entry(i, k):
            change = row_of(alpha, i) * row_of(cols[k], j) + row_of(beta, i) * row_of(cols[k], j + 1)
            return row_of(cols[k], i) - inv * change

        if j + 2 < PANEL:
            a, b, c = entry(j + 2, j + 2), entry(j + 2, j + 3), entry(j + 3, j + 3)
        for k in range(PANEL):
            if k in (j, j + 1):
                continue
            top, low = row_of(cols[k], j), row_of(cols[k], j + 1)
            cols[k] = jnp.where(both, 0.0, cols[k]) - inv * (alpha * top + beta * low)
            if k < j:
                factor[k] = jnp.where(
                    first, top * root_a, jnp.where(second, (low - ratio * top) * root_c, factor[k])
                )
        factor[j] = jnp.where(first, root_a, jnp.where(second, -(ratio * root_c), factor[j]))
        factor[j + 1] = jnp.where(second, root_c, factor[j + 1])
        cols[j] = -(inv * alpha)
        cols[j + 1] = -(inv * beta)
    return cols, factor


def combine(cols, value):
    return added([cols[j] * row_of(value, j) for j in range(PANEL)])


def block_inverse_factor(groups, tasks):
    row = lax.broadcasted_iota(jnp.int32, (PANEL, BLOCK), 0)
    lane = lax.broadcasted_iota(jnp.int32, (PANEL, BLOCK), 1)
    block = [lanes_of(groups[0], j) for j in range(PANEL)]
    for k in range(PANELS):
        base = k * PANEL
        inside = (lane >= base) & (lane < base + PANEL)
        full, factor = small_inverse(block, row)
        panel = jnp.where(inside, (lane == row + base).astype(jnp.float32), groups[k])
        if k + 1 < PANELS:
            down = [lanes_of(groups[k + 1], base + j) for j in range(PANEL)]
            block = []
            for m in range(base + PANEL, base + PANEL + AHEAD):
                column = combine(full, lanes_of(groups[k], m))
                block.append(lanes_of(groups[k + 1], m) - combine(down, column))
            solved = combine(full, panel)
            rows = [row_of(solved, j) for j in range(PANEL)]
            for i in range(k + 1, PANELS):
                old = groups[i]
                change = added([lanes_of(old, base + j) * rows[j] for j in range(PANEL)])
                groups[i] = jnp.where(inside, 0.0, old) - change
            for m in range(base + PANEL + AHEAD, base + 2 * PANEL):
                block.append(lanes_of(groups[k + 1], m))
        groups[k] = jnp.where(lane <= row + base, combine(factor, panel), 0.0)
        if k < len(tasks):
            tasks[k]()
    return groups


def split_halves(value):
    high = value.astype(jnp.bfloat16)
    low = (value - high.astype(jnp.float32)).astype(jnp.bfloat16)
    return high, low


def wide_terms(value):
    high, low = split_halves(value)
    return jnp.concatenate([high, high, low], axis=1)


def product(terms, right):
    high, low = split_halves(right)
    return jnp.dot(
        terms, jnp.concatenate([high, low, high], axis=0), preferred_element_type=jnp.float32
    )


def later_products(work_ref, k, inverse, columns):
    before, through = slice(0, k * BLOCK), slice(0, (k + 1) * BLOCK)
    lefts = {}

    def solve(j):
        upper = product(inverse, work_ref[k, :, columns(j)])
        work_ref[k, :, columns(j)] = upper
        lefts[j] = wide_terms(upper.T)

    def solve_before():
        work_ref[k, :, before] = product(inverse, work_ref[k, :, before])

    def update(i, j):
        work_ref[i, :, columns(j)] -= product(lefts[i], work_ref[k, :, columns(j)])

    def update_before(i):
        change = product(lefts[i], work_ref[k, :, through])
        if k > 0:
            work_ref[i, :, before] -= change[:, before]
        work_ref[i, :, columns(k)] = -change[:, columns(k)]

    rest = range(k + 1, BLOCKS)
    tasks = [functools.partial(solve, j) for j in rest[1:]]
    if k > 0:
        tasks.append(solve_before)
    for i in rest:
        tasks += [functools.partial(update, i, j) for j in range(i, BLOCKS) if j > k + 1]
        tasks.append(functools.partial(update_before, i))
    if k + 1 < BLOCKS:
        solve(k + 1)
        update(k + 1, k + 1)
        return tasks
    for task in tasks:
        task()
    return []


def factor_kernel(where_ref, own_ref, one_ref, two_ref, three_ref, out_ref, slab_ref, work_ref):
    here = where_ref[0]
    for back, ref in enumerate((own_ref, one_ref, two_ref, three_ref)):
        slab_ref[lax.rem(here + (BLOCKS - back), BLOCKS)] = ref[...]

    def block(i, j):
        if j - i < KEPT:
            return slab_ref[i, :, (j - i) * BLOCK : (j - i + 1) * BLOCK]
        return slab_ref[j, :, (BLOCKS + i - j) * BLOCK : (BLOCKS + i - j + 1) * BLOCK].T

    most = jnp.maximum(
        jnp.maximum(block(0, 0), block(1, 1)), jnp.maximum(block(2, 2), block(3, 3))
    )
    most = jnp.max(jnp.max(most, axis=0, keepdims=True), axis=1, keepdims=True)
    scale = 1.0 / most
    for i in range(BLOCKS):
        for j in range(i, BLOCKS):
            work_ref[i, :, j * BLOCK : (j + 1) * BLOCK] = block(i, j) * scale
    back_scale = lax.rsqrt(most)

    def columns(j):
        return slice(j * BLOCK, (j + 1) * BLOCK)

    tasks = []
    for k in range(BLOCKS):
        at, to = k * BLOCK, (k + 1) * BLOCK
        groups = [work_ref[k, i * PANEL : (i + 1) * PANEL, at:to] for i in range(PANELS)]
        inverse = jnp.concatenate(block_inverse_factor(groups, tasks), axis=0)
        work_ref[k, :, at:to] = inverse
        tasks = later_products(work_ref, k, wide_terms(inverse), columns)
    for i in range(BLOCKS):
        to = (i + 1) * BLOCK
        rows = slice(i * BLOCK, to)
        out_ref[rows, :to] = (work_ref[i, :, :to] * back_scale).astype(jnp.bfloat16)
        if to < RANK:
            out_ref[rows, to:] = jnp.zeros((BLOCK, RANK - to), jnp.bfloat16)


def inverse_factor(where, slabs):
    vmem = pl.BlockSpec(memory_space=pltpu.VMEM)
    return pl.pallas_call(
        factor_kernel,
        out_shape=jax.ShapeDtypeStruct((RANK, RANK), jnp.bfloat16),
        in_specs=[pl.BlockSpec(memory_space=pltpu.SMEM)] + [vmem] * BLOCKS,
        out_specs=vmem,
        scratch_shapes=[
            pltpu.VMEM((BLOCKS, BLOCK, KEPT * BLOCK), jnp.float32),
            pltpu.VMEM((BLOCKS, BLOCK, RANK), jnp.float32),
        ],
        compiler_params=pltpu.CompilerParams(vmem_limit_bytes=24 * 1024 * 1024),
        cost_estimate=pl.CostEstimate(flops=2 * 10**10, bytes_accessed=0, transcendentals=0),
    )(where, *slabs)


SIZES = {"x": X_SIZE, "z": Z_SIZE, "y": BLOCKS, "core": 2}


def spread(chunks, axis):
    return lax.all_to_all(chunks, axis, split_axis=0, concat_axis=0, tiled=True)


def swap(value, axis, mask=1):
    return lax.ppermute(value, axis, [(i, i ^ mask) for i in range(SIZES[axis])])


def quad(value, axis):
    return [value] + [swap(value, axis, step) for step in (1, 2, 3)]


def pick(first, value, other):
    return jnp.stack([jnp.where(first, value, other), jnp.where(first, other, value)])


def item(stack, index):
    return lax.dynamic_index_in_dim(stack, index, 0, keepdims=False)


def x_terms(value, plane):
    pieces = value.reshape(X_SIZE, value.shape[0] // X_SIZE, value.shape[1])
    terms = [item(pieces, plane)]
    for step in range(1, X_SIZE):
        send = item(pieces, lax.bitwise_xor(plane, np.uint32(step)))
        terms.append(swap(send, "x", step))
    return terms


def local(momentum, gradient, basis_in):
    experts, rows, cols = momentum.shape
    rank = basis_in.shape[-1]
    expert = lax.axis_index("core").astype(jnp.uint32)
    place = lax.axis_index("y").astype(jnp.uint32)
    plane = lax.axis_index("x").astype(jnp.uint32)
    first = expert == 0
    buffer = lax.optimization_barrier(momentum + gradient.astype(jnp.float32))
    half = buffer.astype(jnp.bfloat16)
    partial = jnp.einsum(
        "erc,eck->erk", half, basis_in, preferred_element_type=jnp.float32
    ).astype(jnp.bfloat16)
    term = item(partial, expert) + swap(item(partial, 1 - expert), "core")
    upper, lower = term[: rows // 2], term[rows // 2 :]
    upper, lower = upper + swap(upper, "y", 1), lower + swap(lower, "y", 3)
    upper, lower = upper + swap(upper, "y", 3), lower + swap(lower, "y", 1)
    projected = jnp.concatenate([upper, lower], axis=0)

    turned = lax.dynamic_slice_in_dim(
        jnp.concatenate([projected, projected[:, : (KEPT - 1) * BLOCK]], axis=1),
        place * np.uint32(BLOCK),
        KEPT * BLOCK,
        axis=1,
    )
    gram = jnp.einsum("rk,rl->kl", turned[:, :BLOCK], turned, preferred_element_type=jnp.float32)
    gram = added(x_terms(gram, plane))

    gram = gram + swap(gram, "z", 4)
    gram = added(quad(gram, "z"))
    parts = quad(gram, "x")
    low = lax.bitwise_and(plane, np.uint32(1)) == 0
    slab = pick(
        plane < np.uint32(2), pick(low, parts[0], parts[1]), pick(low, parts[2], parts[3])
    ).reshape(BLOCK, KEPT * BLOCK)
    slabs = [slab]
    for step in range(1, BLOCKS):
        slabs.append(lax.ppermute(slab, "y", [(i, (i + step) % BLOCKS) for i in range(BLOCKS)]))

    whole = jnp.stack([item(half, expert), swap(item(half, 1 - expert), "core")])
    wide = jnp.einsum("hrc,rk->hck", whole, projected, preferred_element_type=jnp.float32)
    row_count = X_SIZE * Z_SIZE
    wide = wide.astype(jnp.bfloat16).reshape(row_count, 2 * cols // row_count, rank)
    wide = jnp.sum(spread(wide, ("x", "z")).astype(jnp.float32), axis=0).astype(jnp.bfloat16)
    wide = spread(jnp.broadcast_to(wide[None], (row_count,) + wide.shape), ("x", "z"))

    inverse = inverse_factor(jnp.reshape(place, (1,)).astype(jnp.int32), slabs)

    def solve(value):
        return jnp.einsum("rk,lk->rl", value, inverse, preferred_element_type=jnp.float32)

    reduced = solve(wide.reshape(2 * cols, rank))
    squares = added(quad(jnp.sum(reduced * reduced, axis=0, keepdims=True), "y"))
    orthonormal = solve(projected).astype(jnp.bfloat16)

    def outer(right):
        value = jnp.einsum("rk,ck->rc", orthonormal, right, preferred_element_type=jnp.float32)
        return value[:, :cols], value[:, cols:]

    own, other = outer(reduced.astype(jnp.bfloat16))
    other = swap((0.1 * other).astype(jnp.bfloat16), "core")
    momentum_new = buffer - pick(first, 0.1 * own, other.astype(jnp.float32))
    new_basis = (reduced * lax.rsqrt(squares + 1e-06)).astype(jnp.bfloat16)
    update_scale = math.sqrt(ROWS * COLS / RANK)
    own, other = outer(new_basis)
    own = (update_scale * own).astype(jnp.bfloat16)
    other = swap((update_scale * other).astype(jnp.bfloat16), "core")
    return (momentum_new, pick(first, own, other))


def solution(mesh):
    lines = Mesh(mesh.devices.reshape(X_SIZE, Z_SIZE, BLOCKS, 2), ("x", "z", "y", "core"))
    placed = P(None, ("x", "z"), ("y", "core"))
    return jax.shard_map(
        local,
        mesh=lines,
        in_specs=(placed, placed, P(None, ("y", "core"), None)),
        out_specs=(placed, placed),
        check_vma=False,
    )
```

```python
import functools
import math

import jax
import jax.numpy as jnp
import numpy as np
from jax import lax
from jax.experimental import pallas as pl
from jax.experimental.pallas import tpu as pltpu
from jax.sharding import Mesh
from jax.sharding import PartitionSpec as P

ROWS = 7168
COLS = 2048
RANK = 512
BLOCK = 128
PANEL = 8
BLOCKS = RANK // BLOCK
PANELS = BLOCK // PANEL
KEPT = 3
AHEAD = 8
X_SIZE = 4
Z_SIZE = 8


def lanes_of(value, lane):
    return jnp.broadcast_to(value[:, lane : lane + 1], (PANEL, BLOCK))


def row_of(value, row):
    return jnp.broadcast_to(value[row : row + 1, :], (PANEL, BLOCK))


def added(terms):
    while len(terms) > 1:
        terms = [terms[i] + terms[i + 1] for i in range(0, len(terms), 2)]
    return terms[0]


def small_inverse(cols, pivots, row):
    cols = list(cols)
    factor = [jnp.zeros((PANEL, BLOCK), jnp.float32) for _ in range(PANEL)]
    for j in range(0, PANEL, 2):
        first, second = row == j, row == j + 1
        both = first | second
        left, right = cols[j], cols[j + 1]
        if j == 0:
            a, b, c = pivots
        root = lax.rsqrt(a * c - b * b)
        inv = root * root
        root_a = lax.rsqrt(a)
        ratio = b * (root_a * root_a)
        root_c = lax.rsqrt(c - b * ratio)
        left = jnp.where(first, -1.0, jnp.where(second, 0.0, left))
        right = jnp.where(first, 0.0, jnp.where(second, -1.0, right))
        alpha, beta = left * c - right * b, right * a - left * b

        def entry(i, k):
            change = row_of(alpha, i) * row_of(cols[k], j) + row_of(beta, i) * row_of(cols[k], j + 1)
            return row_of(cols[k], i) - inv * change

        if j + 2 < PANEL:
            a, b, c = entry(j + 2, j + 2), entry(j + 2, j + 3), entry(j + 3, j + 3)
        for k in range(PANEL):
            if k in (j, j + 1):
                continue
            top, low = row_of(cols[k], j), row_of(cols[k], j + 1)
            cols[k] = jnp.where(both, 0.0, cols[k]) - inv * (alpha * top + beta * low)
            if k < j:
                factor[k] = jnp.where(
                    first, top * root_a, jnp.where(second, (low - ratio * top) * root_c, factor[k])
                )
        factor[j] = jnp.where(first, root_a, jnp.where(second, -(ratio * root_c), factor[j]))
        factor[j + 1] = jnp.where(second, root_c, factor[j + 1])
        cols[j] = -(inv * alpha)
        cols[j + 1] = -(inv * beta)
    return cols, factor


def combine(cols, value):
    return added([cols[j] * row_of(value, j) for j in range(PANEL)])


def block_inverse_factor(groups, tasks):
    row = lax.broadcasted_iota(jnp.int32, (PANEL, BLOCK), 0)
    lane = lax.broadcasted_iota(jnp.int32, (PANEL, BLOCK), 1)
    block = [lanes_of(groups[0], j) for j in range(PANEL)]
    pivots = row_of(block[0], 0), row_of(block[1], 0), row_of(block[1], 1)
    for k in range(PANELS):
        base = k * PANEL
        inside = (lane >= base) & (lane < base + PANEL)
        full, factor = small_inverse(block, pivots, row)
        panel = jnp.where(inside, (lane == row + base).astype(jnp.float32), groups[k])
        if k + 1 < PANELS:
            down = [lanes_of(groups[k + 1], base + j) for j in range(PANEL)]
            block = []
            solved_cols = []
            for m in range(base + PANEL, base + PANEL + AHEAD):
                column = combine(full, lanes_of(groups[k], m))
                solved_cols.append(column)
                block.append(lanes_of(groups[k + 1], m) - combine(down, column))

            def entry(i, m):
                change = combine([row_of(part, i) for part in down], solved_cols[m])
                return row_of(lanes_of(groups[k + 1], base + PANEL + m), i) - change

            pivots = entry(0, 0), entry(0, 1), entry(1, 1)
            solved = combine(full, panel)
            rows = [row_of(solved, j) for j in range(PANEL)]
            for i in range(k + 1, PANELS):
                old = groups[i]
                change = added([lanes_of(old, base + j) * rows[j] for j in range(PANEL)])
                groups[i] = jnp.where(inside, 0.0, old) - change
            for m in range(base + PANEL + AHEAD, base + 2 * PANEL):
                block.append(lanes_of(groups[k + 1], m))
        groups[k] = jnp.where(lane <= row + base, combine(factor, panel), 0.0)
        if k < len(tasks):
            tasks[k]()
    return groups


def split_halves(value):
    high = value.astype(jnp.bfloat16)
    low = (value - high.astype(jnp.float32)).astype(jnp.bfloat16)
    return high, low


def wide_terms(value):
    high, low = split_halves(value)
    return jnp.concatenate([high, high, low], axis=1)


def product(terms, right):
    high, low = split_halves(right)
    return jnp.dot(
        terms, jnp.concatenate([high, low, high], axis=0), preferred_element_type=jnp.float32
    )


def later_products(work_ref, k, inverse, columns):
    before, through = slice(0, k * BLOCK), slice(0, (k + 1) * BLOCK)
    lefts = {}

    def solve(j):
        upper = product(inverse, work_ref[k, :, columns(j)])
        work_ref[k, :, columns(j)] = upper
        lefts[j] = wide_terms(upper.T)

    def solve_before():
        work_ref[k, :, before] = product(inverse, work_ref[k, :, before])

    def update(i, j):
        work_ref[i, :, columns(j)] -= product(lefts[i], work_ref[k, :, columns(j)])

    def update_before(i):
        change = product(lefts[i], work_ref[k, :, through])
        if k > 0:
            work_ref[i, :, before] -= change[:, before]
        work_ref[i, :, columns(k)] = -change[:, columns(k)]

    rest = range(k + 1, BLOCKS)
    tasks = [functools.partial(solve, j) for j in rest[1:]]
    if k > 0:
        tasks.append(solve_before)
    for i in rest:
        tasks += [functools.partial(update, i, j) for j in range(i, BLOCKS) if j > k + 1]
        tasks.append(functools.partial(update_before, i))
    if k + 1 < BLOCKS:
        solve(k + 1)
        update(k + 1, k + 1)
        return tasks
    for task in tasks:
        task()
    return []


def factor_kernel(where_ref, own_ref, one_ref, two_ref, three_ref, out_ref, slab_ref, work_ref):
    here = where_ref[0]
    for back, ref in enumerate((own_ref, one_ref, two_ref, three_ref)):
        slab_ref[lax.rem(here + (BLOCKS - back), BLOCKS)] = ref[...]

    def block(i, j):
        if j - i < KEPT:
            return slab_ref[i, :, (j - i) * BLOCK : (j - i + 1) * BLOCK]
        return slab_ref[j, :, (BLOCKS + i - j) * BLOCK : (BLOCKS + i - j + 1) * BLOCK].T

    most = jnp.maximum(
        jnp.maximum(block(0, 0), block(1, 1)), jnp.maximum(block(2, 2), block(3, 3))
    )
    most = jnp.max(jnp.max(most, axis=0, keepdims=True), axis=1, keepdims=True)
    scale = 1.0 / most
    for i in range(BLOCKS):
        for j in range(i, BLOCKS):
            work_ref[i, :, j * BLOCK : (j + 1) * BLOCK] = block(i, j) * scale
    back_scale = lax.rsqrt(most)

    def columns(j):
        return slice(j * BLOCK, (j + 1) * BLOCK)

    tasks = []
    for k in range(BLOCKS):
        at, to = k * BLOCK, (k + 1) * BLOCK
        groups = [work_ref[k, i * PANEL : (i + 1) * PANEL, at:to] for i in range(PANELS)]
        inverse = jnp.concatenate(block_inverse_factor(groups, tasks), axis=0)
        work_ref[k, :, at:to] = inverse
        tasks = later_products(work_ref, k, wide_terms(inverse), columns)
    for i in range(BLOCKS):
        to = (i + 1) * BLOCK
        rows = slice(i * BLOCK, to)
        out_ref[rows, :to] = (work_ref[i, :, :to] * back_scale).astype(jnp.bfloat16)
        if to < RANK:
            out_ref[rows, to:] = jnp.zeros((BLOCK, RANK - to), jnp.bfloat16)


def inverse_factor(where, slabs):
    vmem = pl.BlockSpec(memory_space=pltpu.VMEM)
    return pl.pallas_call(
        factor_kernel,
        out_shape=jax.ShapeDtypeStruct((RANK, RANK), jnp.bfloat16),
        in_specs=[pl.BlockSpec(memory_space=pltpu.SMEM)] + [vmem] * BLOCKS,
        out_specs=vmem,
        scratch_shapes=[
            pltpu.VMEM((BLOCKS, BLOCK, KEPT * BLOCK), jnp.float32),
            pltpu.VMEM((BLOCKS, BLOCK, RANK), jnp.float32),
        ],
        compiler_params=pltpu.CompilerParams(vmem_limit_bytes=24 * 1024 * 1024),
        cost_estimate=pl.CostEstimate(flops=2 * 10**10, bytes_accessed=0, transcendentals=0),
    )(where, *slabs)


SIZES = {"x": X_SIZE, "z": Z_SIZE, "y": BLOCKS, "core": 2}


def spread(chunks, axis):
    return lax.all_to_all(chunks, axis, split_axis=0, concat_axis=0, tiled=True)


def swap(value, axis, mask=1):
    return lax.ppermute(value, axis, [(i, i ^ mask) for i in range(SIZES[axis])])


def quad(value, axis):
    return [value] + [swap(value, axis, step) for step in (1, 2, 3)]


def pick(first, value, other):
    return jnp.stack([jnp.where(first, value, other), jnp.where(first, other, value)])


def item(stack, index):
    return lax.dynamic_index_in_dim(stack, index, 0, keepdims=False)


def x_terms(value, plane):
    pieces = value.reshape(X_SIZE, value.shape[0] // X_SIZE, value.shape[1])
    terms = [item(pieces, plane)]
    for step in range(1, X_SIZE):
        send = item(pieces, lax.bitwise_xor(plane, np.uint32(step)))
        terms.append(swap(send, "x", step))
    return terms


def local(momentum, gradient, basis_in):
    experts, rows, cols = momentum.shape
    rank = basis_in.shape[-1]
    expert = lax.axis_index("core").astype(jnp.uint32)
    place = lax.axis_index("y").astype(jnp.uint32)
    plane = lax.axis_index("x").astype(jnp.uint32)
    first = expert == 0
    buffer = lax.optimization_barrier(momentum + gradient.astype(jnp.float32))
    half = buffer.astype(jnp.bfloat16)
    partial = jnp.einsum(
        "erc,eck->erk", half, basis_in, preferred_element_type=jnp.float32
    ).astype(jnp.bfloat16)
    term = item(partial, expert) + swap(item(partial, 1 - expert), "core")
    upper, lower = term[: rows // 2], term[rows // 2 :]
    upper, lower = upper + swap(upper, "y", 1), lower + swap(lower, "y", 3)
    upper, lower = upper + swap(upper, "y", 3), lower + swap(lower, "y", 1)
    projected = jnp.concatenate([upper, lower], axis=0)

    turned = lax.dynamic_slice_in_dim(
        jnp.concatenate([projected, projected[:, : (KEPT - 1) * BLOCK]], axis=1),
        place * np.uint32(BLOCK),
        KEPT * BLOCK,
        axis=1,
    )
    gram = jnp.einsum("rk,rl->kl", turned[:, :BLOCK], turned, preferred_element_type=jnp.float32)
    gram = added(x_terms(gram, plane))

    gram = gram + swap(gram, "z", 4)
    gram = added(quad(gram, "z"))
    parts = quad(gram, "x")
    low = lax.bitwise_and(plane, np.uint32(1)) == 0
    slab = pick(
        plane < np.uint32(2), pick(low, parts[0], parts[1]), pick(low, parts[2], parts[3])
    ).reshape(BLOCK, KEPT * BLOCK)
    slabs = [slab]
    for step in range(1, BLOCKS):
        slabs.append(lax.ppermute(slab, "y", [(i, (i + step) % BLOCKS) for i in range(BLOCKS)]))

    whole = jnp.stack([item(half, expert), swap(item(half, 1 - expert), "core")])
    wide = jnp.einsum("hrc,rk->hck", whole, projected, preferred_element_type=jnp.float32)
    row_count = X_SIZE * Z_SIZE
    wide = wide.astype(jnp.bfloat16).reshape(row_count, 2 * cols // row_count, rank)
    wide = jnp.sum(spread(wide, ("x", "z")).astype(jnp.float32), axis=0).astype(jnp.bfloat16)
    wide = spread(jnp.broadcast_to(wide[None], (row_count,) + wide.shape), ("x", "z"))

    inverse = inverse_factor(jnp.reshape(place, (1,)).astype(jnp.int32), slabs)

    def solve(value):
        return jnp.einsum("rk,lk->rl", value, inverse, preferred_element_type=jnp.float32)

    reduced = solve(wide.reshape(2 * cols, rank))
    squares = added(quad(jnp.sum(reduced * reduced, axis=0, keepdims=True), "y"))
    orthonormal = solve(projected).astype(jnp.bfloat16)

    def outer(right):
        value = jnp.einsum("rk,ck->rc", orthonormal, right, preferred_element_type=jnp.float32)
        return value[:, :cols], value[:, cols:]

    own, other = outer(reduced.astype(jnp.bfloat16))
    other = swap((0.1 * other).astype(jnp.bfloat16), "core")
    momentum_new = buffer - pick(first, 0.1 * own, other.astype(jnp.float32))
    new_basis = (reduced * lax.rsqrt(squares + 1e-06)).astype(jnp.bfloat16)
    update_scale = math.sqrt(ROWS * COLS / RANK)
    own, other = outer(new_basis)
    own = (update_scale * own).astype(jnp.bfloat16)
    other = swap((update_scale * other).astype(jnp.bfloat16), "core")
    return (momentum_new, pick(first, own, other))


def solution(mesh):
    lines = Mesh(mesh.devices.reshape(X_SIZE, Z_SIZE, BLOCKS, 2), ("x", "z", "y", "core"))
    placed = P(None, ("x", "z"), ("y", "core"))
    return jax.shard_map(
        local,
        mesh=lines,
        in_specs=(placed, placed, P(None, ("y", "core"), None)),
        out_specs=(placed, placed),
        check_vma=False,
    )
```
